32 devices in a mesh: elem: 8 (over z, y), mode: 4 (over x, core).
Axes of the slice: x: 2, y: 2, z: 4, core: 2. Of those that a mesh axis runs over, the one named last changes fastest.
Arguments:
- modal_history: float32 [4096, 512], P('elem', 'mode'), may hold values from -6 to 6
- stress_modes: float32 [512, 384], P('mode', 'elem'), may hold values from -0.375 to 0.375
Outputs:
- stress_spectrum: float32 [384, 2, 2048], P(('elem', 'mode'))
The draws below stay inside these ranges and needn't reach their ends.
All inputs are finite; a program needn't handle non-finite values.
Results may differ from the reference program's by a relative error of at most 0.00007.
Values sent between devices are 32-bit elements; how exact they have to be, the bound alone decides.
A program may use at most 64 MiB of HBM per device.

```python
import jax
import jax.numpy as jnp
from jax import lax

M = 512
NT = 4096
C = 6
E = 64


def raised(entries, own_key, source, target, blocks, factor):
    owner, partner = [(jnp.arange(entries.shape[dim]) // (entries.shape[dim] // blocks)).reshape([-1 if axis == dim else 1 for axis in range(entries.ndim)]) for dim in (source, target)]
    chosen = jax.random.permutation(own_key, blocks)[partner]
    strong = (owner == chosen) | (owner == (partner + blocks // 2) % blocks)
    return jnp.where(strong, factor * entries, entries)


def block_levels(rng, extent, cuts, low, top_value):
    factor_of = 1.0
    for axis_at, shards_of in cuts:
        draws = jax.random.uniform(jax.random.fold_in(jax.random.fold_in(rng, 6), axis_at), (shards_of,), jnp.float32, low / len(cuts), top_value / len(cuts))
        factor_of = factor_of * jnp.repeat(jnp.exp(draws), extent[axis_at] // shards_of).reshape((-1,) + (1,) * (len(extent) - 1 - axis_at))
    return factor_of


def gaussian(stream_key, shape, spread, most, pieces=(), dtype=jnp.bfloat16):
    level = block_levels(stream_key, shape, pieces, -0.22, 0.18) if pieces else 1.0
    drawn = jax.random.normal(stream_key, shape, jnp.float32) * spread * level
    return jnp.minimum(jnp.maximum(drawn, -most), most).astype(dtype)


def gaussian_with(own_key, dims, deviation, bound, cuts, heavy, held_as=jnp.bfloat16):
    entries = deviation * jax.random.normal(own_key, dims, jnp.float32)
    if cuts:
        entries = entries * block_levels(own_key, dims, cuts, -0.22, 0.18)
    return jnp.clip(raised(entries, jax.random.fold_in(own_key, 3), *heavy), -bound, bound).astype(held_as)


def setup_inputs(seed: int = 0) -> dict:
    key_of = jax.random.split(jax.random.key(seed), 3)
    return {
        "modal_history": gaussian(key_of[0], (NT, M), 1.0, 6.0, ((0, 8), (1, 4)), jnp.float32),
        "stress_modes": gaussian_with(key_of[1], (M, E * C), M ** -0.5, 0.375, ((0, 4), (1, 8)), (0, 1, 8, 2.0), jnp.float32),
    }


def reference(modal_history, stress_modes):
    stress = jnp.dot(stress_modes.T, modal_history.T, precision=lax.Precision.HIGHEST, preferred_element_type=jnp.float32)
    spectrum = jnp.fft.rfft(stress, axis=1, norm="ortho")[:, : NT // 2]
    return jnp.stack([jnp.real(spectrum), jnp.imag(spectrum)], axis=1).astype(jnp.float32)
```

```python
import functools
import math

import jax
import jax.numpy as jnp
import ml_dtypes
import numpy as np
from jax import lax
from jax.experimental import pallas as pl
from jax.experimental.pallas import tpu as pltpu
from jax.sharding import PartitionSpec as P

highest = lax.Precision.HIGHEST
MESH = pl.DeviceIdType.MESH
f32, bf16 = jnp.float32, jnp.bfloat16

RADIX = 128
REST = 32


def spectra(signal):
    columns = signal.shape[0]
    radix = 64
    halved = radix // 2
    blocked = signal.reshape(columns, radix, radix)
    counter = jnp.arange(radix, dtype=jnp.int32)
    products = counter[:, None] * counter[None, :]
    small_angle = (products % radix).astype(jnp.float32) * (2.0 * math.pi / radix)
    cosine_small = jnp.cos(small_angle)
    sine_small = jnp.sin(small_angle)
    twist_angle = (products % (radix * radix)).astype(jnp.float32) * (
        2.0 * math.pi / (radix * radix)
    )
    twist_cos = jnp.cos(twist_angle)
    twist_sin = jnp.sin(twist_angle)
    first_real = jnp.einsum("cab,ak->cbk", blocked, cosine_small, precision=highest)
    first_imag = -jnp.einsum("cab,ak->cbk", blocked, sine_small, precision=highest)
    turned_real = first_real * twist_cos + first_imag * twist_sin
    turned_imag = first_imag * twist_cos - first_real * twist_sin
    cosine_half = cosine_small[:, :halved]
    sine_half = sine_small[:, :halved]
    final_real = jnp.einsum(
        "cbk,bj->cjk", turned_real, cosine_half, precision=highest
    ) + jnp.einsum("cbk,bj->cjk", turned_imag, sine_half, precision=highest)
    final_imag = jnp.einsum(
        "cbk,bj->cjk", turned_imag, cosine_half, precision=highest
    ) - jnp.einsum("cbk,bj->cjk", turned_real, sine_half, precision=highest)
    stacked = jnp.stack([final_real, final_imag], axis=1) * (1.0 / radix)
    return stacked.reshape(columns, 2, halved * radix)


def plain(modal_history, stress_modes):
    elem_count = lax.axis_size("elem")
    mode_count = lax.axis_size("mode")
    local_steps = modal_history.shape[0]
    partial_value = jnp.einsum(
        "mp,tm->pt",
        lax.all_gather(stress_modes, "elem", axis=1, tiled=True),
        modal_history,
        precision=highest,
        preferred_element_type=jnp.float32,
    )
    owned_width = partial_value.shape[0] // (elem_count * mode_count)
    reordered = partial_value.reshape(elem_count, mode_count, owned_width, local_steps)
    reordered = reordered.transpose(1, 0, 2, 3).reshape(
        mode_count * elem_count * owned_width, local_steps
    )
    summed = lax.psum_scatter(reordered, "mode", scatter_dimension=0, tiled=True)
    stress = lax.all_to_all(summed, "elem", split_axis=0, concat_axis=1, tiled=True)
    return spectra(stress)


def split_np(x):
    hi = x.astype(np.float32).astype(ml_dtypes.bfloat16)
    lo = (x - hi.astype(np.float64)).astype(np.float32).astype(ml_dtypes.bfloat16)
    return hi, lo


def tables(steps):
    two_pi = 2.0 * np.pi
    a = np.arange(RADIX)
    ang = two_pi * ((a[:, None] * a[None, :]) % RADIX) / RADIX
    first = np.concatenate([np.cos(ang), -np.sin(ang)], axis=1)
    first_hi, first_lo = split_np(first)
    row = np.arange(REST)
    b = (row % 4) * 8 + row // 4
    twist = two_pi * ((b[:, None] * a[None, :]) % steps) / steps
    k2 = np.arange(REST // 2)
    last = two_pi * ((k2[:, None] * b[None, :]) % REST) / REST
    real = np.concatenate([np.cos(last), np.sin(last)], axis=1)
    imag = np.concatenate([-np.sin(last), np.cos(last)], axis=1)
    second = np.stack([real, imag], axis=1).reshape(REST, 2 * REST) / math.sqrt(steps)
    second_hi, second_lo = split_np(second)
    second_all = np.concatenate([second_hi, second_hi, second_lo], axis=1)
    twist_all = np.stack([np.cos(twist), np.sin(twist)]).astype(np.float32)
    return first_hi, first_lo, twist_all, second_all


def split(x):
    hi = x.astype(bf16)
    lo = (x - hi.astype(f32)).astype(bf16)
    return hi, lo


def nt(a, b):
    return lax.dot_general(
        a, b, (((1,), (1,)), ((), ())), preferred_element_type=f32
    )


def nn(a, b):
    return jnp.dot(a, b, preferred_element_type=f32)


def fused(
    elems, modes, width,
    hist, shape_ref, first_hi, first_lo, twist, second,
    out,
    hbuf, s_send, s_recv, gathered, s_all, outbox, inbox, turned,
    own_sem, hs_sem, hr_sem, s1s_sem, s1r_sem, s2s_sem, s2r_sem, as_sem, ar_sem,
):
    chunks = 2
    e = lax.axis_index("elem")
    m = lax.axis_index("mode")
    sibling = m + 1 - 2 * (m % 2)
    across = (m + 2) % modes
    diagonal = (modes - 1) - m

    barrier = pltpu.get_barrier_semaphore()
    for peer in (sibling, across, diagonal):
        pl.semaphore_signal(barrier, inc=1, device_id=(e, peer), device_id_type=MESH)
    for d in range(1, elems):
        pl.semaphore_signal(
            barrier, inc=1, device_id=((e + d) % elems, m), device_id_type=MESH
        )

    own = [
        pltpu.make_async_copy(hist.at[:, c], hbuf.at[m, c], own_sem.at[c])
        for c in range(chunks)
    ]
    for copy in own:
        copy.start()

    modes_t = shape_ref[...].T
    for p in range(modes):
        s_send[p, :width, :] = modes_t[p * width : (p + 1) * width, :]
    s_recv[m, :width, :] = s_send[m, :width, :]
    s_all[...] = jnp.zeros_like(s_all)

    pl.semaphore_wait(barrier, modes - 1 + elems - 1)

    first_copies = []
    for i, peer in enumerate((across, diagonal, sibling)):
        first_copies.append((
            pltpu.make_async_remote_copy(
                s_send.at[peer], s_recv.at[m], s1s_sem.at[i], s1r_sem.at[i],
                device_id=(e, peer), device_id_type=MESH,
            ),
            pltpu.make_async_remote_copy(
                s_send.at[peer], s_recv.at[peer], s1s_sem.at[i], s1r_sem.at[i],
                device_id=(e, peer), device_id_type=MESH,
            ),
        ))
    for copy, _ in first_copies:
        copy.start()

    def history_copy(kind, c, origin, peer):
        src = hist.at[:, c] if kind < 2 else hbuf.at[origin, c]
        return pltpu.make_async_remote_copy(
            src, hbuf.at[origin, c], hs_sem.at[kind, c], hr_sem.at[kind, c],
            device_id=(e, peer), device_id_type=MESH,
        )

    to_across = [history_copy(0, c, m, across) for c in range(chunks)]
    to_sibling = [history_copy(1, c, m, sibling) for c in range(chunks)]
    forward = [history_copy(2, c, across, sibling) for c in range(chunks)]
    from_across = [history_copy(0, c, across, across) for c in range(chunks)]
    from_sibling = [history_copy(1, c, sibling, sibling) for c in range(chunks)]
    from_forward = [history_copy(2, c, diagonal, sibling) for c in range(chunks)]
    for c in range(chunks):
        to_across[c].start()
        to_sibling[c].start()

    for _, landed in first_copies:
        landed.wait_recv()
    for p in range(modes):
        gathered[e, p * width : (p + 1) * width, :] = s_recv[p, :width, :]

    order = sorted(range(1, elems), key=lambda d: -min(d, elems - d))
    second_copies = []
    for d in order:
        peer, source = (e + d) % elems, (e + elems - d) % elems
        copy = pltpu.make_async_remote_copy(
            gathered.at[e], gathered.at[e], s2s_sem.at[d], s2r_sem.at[d],
            device_id=(peer, m), device_id_type=MESH,
        )
        landed = pltpu.make_async_remote_copy(
            gathered.at[source], gathered.at[source], s2s_sem.at[d], s2r_sem.at[d],
            device_id=(peer, m), device_id_type=MESH,
        )
        copy.start()
        second_copies.append((copy, landed))

    for c in range(chunks):
        from_across[c].wait_recv()
        forward[c].start()

    for _, landed in second_copies:
        landed.wait_recv()
    for owner in range(elems):
        for p in range(modes):
            s_all[owner * 16 : owner * 16 + width, p * 128 : (p + 1) * 128] = (
                gathered[owner, p * width : (p + 1) * width, :]
            )
    s_hi, s_lo = split(s_all[...])
    s_both = jnp.concatenate([s_hi, s_lo], axis=0)
    rows = s_hi.shape[0]

    last_copies = []
    for c in range(chunks):
        own[c].wait()
        from_sibling[c].wait_recv()
        from_forward[c].wait_recv()
        pieces = []
        for p in range(modes):
            flat = hbuf.at[p, c].reshape(256, 128)
            pieces.append(
                jnp.concatenate(
                    [flat[pl.ds(i, 16, stride=16), :] for i in range(16)], axis=0
                )
            )
        h_hi, h_lo = split(jnp.concatenate(pieces, axis=1))
        both = nt(s_both, h_hi)
        stress = both[:rows] + (both[rows:] + nt(s_hi, h_lo))
        for owner in range(elems):
            for h in range(2):
                outbox[owner, c, h * width : (h + 1) * width, :] = stress[
                    owner * 16 : owner * 16 + width, h * 128 : (h + 1) * 128
                ]
        for d in order:
            peer, source = (e + d) % elems, (e + elems - d) % elems
            copy = pltpu.make_async_remote_copy(
                outbox.at[peer, c], inbox.at[e, c], as_sem.at[d, c], ar_sem.at[d, c],
                device_id=(peer, m), device_id_type=MESH,
            )
            landed = pltpu.make_async_remote_copy(
                outbox.at[peer, c], inbox.at[source, c], as_sem.at[d, c],
                ar_sem.at[d, c], device_id=(peer, m), device_id_type=MESH,
            )
            copy.start()
            last_copies.append((copy, landed))
        inbox[e, c] = outbox[e, c]

    for _, landed in last_copies:
        landed.wait_recv()

    blocks = [
        jnp.concatenate([inbox[i, 0], inbox[i, 1]], axis=0) for i in range(elems)
    ]
    group = lax.broadcasted_iota(jnp.int32, blocks[0].shape, 1) // 16
    for step in (4, 2, 1):
        low = (group // step) % 2 == 0
        for i in range(elems):
            if (i // step) % 2 == 0:
                one, two = blocks[i], blocks[i + step]
                blocks[i] = jnp.where(low, one, pltpu.roll(two, 16 * step, 1))
                blocks[i + step] = jnp.where(
                    low, pltpu.roll(one, 128 - 16 * step, 1), two
                )
    x_hi, x_lo = split(jnp.concatenate(blocks, axis=0))
    w_hi, w_lo = first_hi[...], first_lo[...]
    once = nn(x_hi, w_hi) + (nn(x_lo, w_hi) + nn(x_hi, w_lo))
    turned[0] = once[:, :128]
    turned[1] = once[:, 128:]

    cos, sin = twist[0], twist[1]
    real, imag = [], []
    for col in range(width):
        re = turned.at[0][pl.ds(col, REST, stride=width), :]
        im = turned.at[1][pl.ds(col, REST, stride=width), :]
        real.append(re * cos + im * sin)
        imag.append(im * cos - re * sin)
    z = jnp.concatenate(
        [jnp.concatenate(real, axis=1), jnp.concatenate(imag, axis=1)], axis=0
    )
    z_hi, z_lo = split(z)
    result = nn(second[...], jnp.concatenate([z_hi, z_lo, z_hi], axis=0))
    for col in range(width):
        out[col] = result[:, col * 128 : (col + 1) * 128]

    for copy, _ in first_copies + second_copies + last_copies:
        copy.wait_send()
    for copy in to_across + to_sibling + forward:
        copy.wait_send()


def with_kernel(modal_history, stress_modes):
    elems, modes = lax.axis_size("elem"), lax.axis_size("mode")
    steps = modal_history.shape[0] * elems
    width = stress_modes.shape[1] // modes
    consts = [jnp.asarray(t) for t in tables(steps)]
    hist = modal_history.reshape(16, 2, 16, 128)
    vmem = pl.BlockSpec(memory_space=pltpu.VMEM)
    dma = pltpu.SemaphoreType.DMA
    result = pl.pallas_call(
        functools.partial(fused, elems, modes, width),
        out_shape=jax.ShapeDtypeStruct((width, REST, RADIX), f32),
        in_specs=[pl.BlockSpec(memory_space=pl.ANY)] + [vmem] * 5,
        out_specs=vmem,
        scratch_shapes=[
            pltpu.VMEM((modes, 2, 16, 16, 128), f32),
            pltpu.VMEM((modes, 16, 128), f32),
            pltpu.VMEM((modes, 16, 128), f32),
            pltpu.VMEM((elems, modes * width, 128), f32),
            pltpu.VMEM((elems * 16, modes * 128), f32),
            pltpu.VMEM((elems, 2, 2 * width, 128), f32),
            pltpu.VMEM((elems, 2, 2 * width, 128), f32),
            pltpu.VMEM((2, REST * width, 128), f32),
            dma((2,)),
            dma((3, 2)), dma((3, 2)),
            dma((3,)), dma((3,)),
            dma((elems,)), dma((elems,)),
            dma((elems, 2)), dma((elems, 2)),
        ],
        compiler_params=pltpu.CompilerParams(
            collective_id=0, has_side_effects=True, vmem_limit_bytes=32 * 1024 * 1024
        ),
    )(hist, stress_modes, *consts)
    ordered = result.reshape(width, REST // 2, 2, RADIX).transpose(0, 2, 1, 3)
    return ordered.reshape(width, 2, REST // 2 * RADIX)


def per_device(modal_history, stress_modes):
    elems, modes = lax.axis_size("elem"), lax.axis_size("mode")
    fits = (
        elems == 8
        and modes == 4
        and modal_history.shape == (512, 128)
        and stress_modes.shape == (128, 48)
    )
    body = with_kernel if fits else plain
    return body(modal_history, stress_modes)


def solution(mesh):
    placed = (P("elem", "mode"), P("mode", "elem"))
    return jax.shard_map(
        per_device,
        mesh=mesh,
        in_specs=placed,
        out_specs=P(("elem", "mode"), None, None),
        check_vma=False,
    )
```

```python
import functools
import math

import jax
import jax.numpy as jnp
import ml_dtypes
import numpy as np
from jax import lax
from jax.experimental import pallas as pl
from jax.experimental.pallas import tpu as pltpu
from jax.sharding import PartitionSpec as P

highest = lax.Precision.HIGHEST
MESH = pl.DeviceIdType.MESH
f32, bf16 = jnp.float32, jnp.bfloat16

RADIX = 128
REST = 32


def spectra(signal):
    columns = signal.shape[0]
    radix = 64
    halved = radix // 2
    blocked = signal.reshape(columns, radix, radix)
    counter = jnp.arange(radix, dtype=jnp.int32)
    products = counter[:, None] * counter[None, :]
    small_angle = (products % radix).astype(jnp.float32) * (2.0 * math.pi / radix)
    cosine_small = jnp.cos(small_angle)
    sine_small = jnp.sin(small_angle)
    twist_angle = (products % (radix * radix)).astype(jnp.float32) * (
        2.0 * math.pi / (radix * radix)
    )
    twist_cos = jnp.cos(twist_angle)
    twist_sin = jnp.sin(twist_angle)
    first_real = jnp.einsum("cab,ak->cbk", blocked, cosine_small, precision=highest)
    first_imag = -jnp.einsum("cab,ak->cbk", blocked, sine_small, precision=highest)
    turned_real = first_real * twist_cos + first_imag * twist_sin
    turned_imag = first_imag * twist_cos - first_real * twist_sin
    cosine_half = cosine_small[:, :halved]
    sine_half = sine_small[:, :halved]
    final_real = jnp.einsum(
        "cbk,bj->cjk", turned_real, cosine_half, precision=highest
    ) + jnp.einsum("cbk,bj->cjk", turned_imag, sine_half, precision=highest)
    final_imag = jnp.einsum(
        "cbk,bj->cjk", turned_imag, cosine_half, precision=highest
    ) - jnp.einsum("cbk,bj->cjk", turned_real, sine_half, precision=highest)
    stacked = jnp.stack([final_real, final_imag], axis=1) * (1.0 / radix)
    return stacked.reshape(columns, 2, halved * radix)


def plain(modal_history, stress_modes):
    elem_count = lax.axis_size("elem")
    mode_count = lax.axis_size("mode")
    local_steps = modal_history.shape[0]
    partial_value = jnp.einsum(
        "mp,tm->pt",
        lax.all_gather(stress_modes, "elem", axis=1, tiled=True),
        modal_history,
        precision=highest,
        preferred_element_type=jnp.float32,
    )
    owned_width = partial_value.shape[0] // (elem_count * mode_count)
    reordered = partial_value.reshape(elem_count, mode_count, owned_width, local_steps)
    reordered = reordered.transpose(1, 0, 2, 3).reshape(
        mode_count * elem_count * owned_width, local_steps
    )
    summed = lax.psum_scatter(reordered, "mode", scatter_dimension=0, tiled=True)
    stress = lax.all_to_all(summed, "elem", split_axis=0, concat_axis=1, tiled=True)
    return spectra(stress)


def split_np(x):
    hi = x.astype(np.float32).astype(ml_dtypes.bfloat16)
    lo = (x - hi.astype(np.float64)).astype(np.float32).astype(ml_dtypes.bfloat16)
    return hi, lo


def tables(steps):
    two_pi = 2.0 * np.pi
    a = np.arange(RADIX)
    ang = two_pi * ((a[:, None] * a[None, :]) % RADIX) / RADIX
    parts = [np.cos(ang), -np.sin(ang)]
    k2 = np.arange(REST // 2)
    for c in range(2):
        row = np.arange(REST // 2)
        b = (2 * c + row % 2) * 8 + row // 2
        twist = two_pi * ((b[:, None] * a[None, :]) % steps) / steps
        parts += [np.cos(twist), np.sin(twist)]
        last = two_pi * ((k2[:, None] * b[None, :]) % REST) / REST
        real = np.concatenate([np.cos(last), np.sin(last)], axis=1)
        imag = np.concatenate([-np.sin(last), np.cos(last)], axis=1)
        second = np.stack([real, imag], axis=1).reshape(REST, REST) / math.sqrt(steps)
        hi, lo = (p.astype(np.float64) for p in split_np(second))
        parts.append(np.concatenate([hi, hi, lo, np.zeros_like(hi)], axis=1))
    return np.concatenate(parts, axis=0).astype(np.float32)


def split(x):
    hi = x.astype(bf16)
    lo = (x - hi.astype(f32)).astype(bf16)
    return hi, lo


def nt(a, b):
    return lax.dot_general(
        a, b, (((1,), (1,)), ((), ())), preferred_element_type=f32
    )


def nn(a, b):
    return jnp.dot(a, b, preferred_element_type=f32)


def fused(
    elems, modes, width,
    hist, shapes, table,
    out,
    hbuf, h_his, h_los, own_shapes, s_send, s_recv, gathered, s_all, outbox, inbox,
    turned, consts,
    own_sem, fetch_sem, hs_sem, hr_sem, s1s_sem, s1r_sem, s2s_sem, s2r_sem,
    as_sem, ar_sem,
):
    chunks = 2
    e = lax.axis_index("elem")
    m = lax.axis_index("mode")
    sibling = m + 1 - 2 * (m % 2)
    across = (m + 2) % modes
    diagonal = (modes - 1) - m
    beside = e + 1 - 2 * (e % 2)

    fetch_shapes = pltpu.make_async_copy(shapes, own_shapes, fetch_sem.at[0])
    fetch_table = pltpu.make_async_copy(table, consts, fetch_sem.at[1])
    own = [
        pltpu.make_async_copy(hist.at[:, c], hbuf.at[m, c], own_sem.at[c])
        for c in range(chunks)
    ]
    fetch_shapes.start()
    for copy in own:
        copy.start()
    fetch_table.start()

    barrier = pltpu.get_barrier_semaphore()
    for d in range(1, elems):
        pl.semaphore_signal(
            barrier, inc=1, device_id=((e + d) % elems, m), device_id_type=MESH
        )
    for peer in (across, diagonal, sibling):
        pl.semaphore_signal(barrier, inc=1, device_id=(e, peer), device_id_type=MESH)

    s_all[...] = jnp.zeros_like(s_all)
    fetch_shapes.wait()
    for p in range(modes):
        s_send[p, :width, :] = own_shapes[p * width : (p + 1) * width, :]
    s_recv[m, :width, :] = s_send[m, :width, :]

    pl.semaphore_wait(barrier, modes - 1 + elems - 1)

    first_copies = []
    for i, peer in enumerate((across, diagonal, sibling)):
        first_copies.append((
            pltpu.make_async_remote_copy(
                s_send.at[peer], s_recv.at[m], s1s_sem.at[i], s1r_sem.at[i],
                device_id=(e, peer), device_id_type=MESH,
            ),
            pltpu.make_async_remote_copy(
                s_send.at[peer], s_recv.at[peer], s1s_sem.at[i], s1r_sem.at[i],
                device_id=(e, peer), device_id_type=MESH,
            ),
        ))
    for copy, _ in first_copies:
        copy.start()

    def history_copy(kind, c, origin, peer):
        src = hist.at[:, c] if kind < 2 else hbuf.at[origin, c]
        return pltpu.make_async_remote_copy(
            src, hbuf.at[origin, c], hs_sem.at[kind, c], hr_sem.at[kind, c],
            device_id=(e, peer), device_id_type=MESH,
        )

    to_across = [history_copy(0, c, m, across) for c in range(chunks)]
    to_sibling = [history_copy(1, c, m, sibling) for c in range(chunks)]
    forward = [history_copy(2, c, across, sibling) for c in range(chunks)]
    from_across = [history_copy(0, c, across, across) for c in range(chunks)]
    from_sibling = [history_copy(1, c, sibling, sibling) for c in range(chunks)]
    from_forward = [history_copy(2, c, diagonal, sibling) for c in range(chunks)]
    for c in range(chunks):
        to_across[c].start()
        to_sibling[c].start()

    def split_history(origin, c):
        flat = hbuf.at[origin, c].reshape(256, 128)
        turned_rows = [flat[pl.ds(i, 16, stride=16), :] for i in range(16)]
        hi, lo = split(jnp.concatenate(turned_rows, axis=0))
        h_his[c, origin] = hi
        h_los[c, origin] = lo

    own[0].wait()
    split_history(m, 0)

    for _, landed in first_copies:
        landed.wait_recv()
    for p in range(modes):
        gathered[e, p * width : (p + 1) * width, :] = s_recv[p, :width, :]

    def shape_copy(slot, block, peer):
        return pltpu.make_async_remote_copy(
            gathered.at[block], gathered.at[block], s2s_sem.at[slot], s2r_sem.at[slot],
            device_id=(peer, m), device_id_type=MESH,
        )

    shape_sends = []
    steps_z = [elems // 2] + [d for d in range(2, elems, 2) if d != elems // 2]
    for d in steps_z:
        shape_sends.append(shape_copy(d, e, (e + d) % elems))
    shape_sends.append(shape_copy(1, e, beside))
    for copy in shape_sends:
        copy.start()

    own[1].wait()
    split_history(m, 1)
    for c in range(chunks):
        from_sibling[c].wait_recv()
        split_history(sibling, c)

    for d in sorted(steps_z, key=lambda d: min(d, elems - d)):
        source = (e + elems - d) % elems
        shape_copy(d, source, source).wait_recv()
        copy = shape_copy(d + 1, source, beside)
        copy.start()
        shape_sends.append(copy)

    from_across[0].wait_recv()
    forward[0].start()
    split_history(across, 0)

    shape_copy(1, beside, beside).wait_recv()
    for d in steps_z:
        shape_copy(d + 1, (beside + elems - d) % elems, beside).wait_recv()
    for owner in range(elems):
        for p in range(modes):
            s_all[owner * 16 : owner * 16 + width, p * 128 : (p + 1) * 128] = (
                gathered[owner, p * width : (p + 1) * width, :]
            )
    s_hi, s_lo = split(s_all[...])
    s_both = jnp.concatenate([s_hi, s_lo], axis=0)
    rows = s_hi.shape[0]

    order = sorted(range(1, elems), key=lambda d: -min(d, elems - d))
    last_copies = []
    for c in range(chunks):
        if c:
            from_across[c].wait_recv()
            forward[c].start()
            split_history(across, c)
        from_forward[c].wait_recv()
        split_history(diagonal, c)
        h_hi = jnp.concatenate([h_his[c, p] for p in range(modes)], axis=1)
        h_lo = jnp.concatenate([h_los[c, p] for p in range(modes)], axis=1)
        both = nt(s_both, h_hi)
        stress = both[:rows] + (both[rows:] + nt(s_hi, h_lo))
        for owner in range(elems):
            for h in range(2):
                outbox[owner, c, h * width : (h + 1) * width, :] = stress[
                    owner * 16 : owner * 16 + width, h * 128 : (h + 1) * 128
                ]
        for d in order:
            peer, source = (e + d) % elems, (e + elems - d) % elems
            copy = pltpu.make_async_remote_copy(
                outbox.at[peer, c], inbox.at[e, c], as_sem.at[d, c], ar_sem.at[d, c],
                device_id=(peer, m), device_id_type=MESH,
            )
            landed = pltpu.make_async_remote_copy(
                outbox.at[peer, c], inbox.at[source, c], as_sem.at[d, c],
                ar_sem.at[d, c], device_id=(peer, m), device_id_type=MESH,
            )
            copy.start()
            last_copies.append((c, copy, landed))
        inbox[e, c] = outbox[e, c]

    fetch_table.wait()
    w_hi, w_lo = split(
        jnp.concatenate([consts[:128, :], consts[128:256, :]], axis=1)
    )
    half = REST // 2
    total = None
    for c in range(chunks):
        for chunk, _, landed in last_copies:
            if chunk == c:
                landed.wait_recv()
        blocks = [inbox[i, c] for i in range(elems)]
        group = lax.broadcasted_iota(jnp.int32, blocks[0].shape, 1) // 16
        for step in (4, 2, 1):
            low = (group // step) % 2 == 0
            for i in range(elems):
                if (i // step) % 2 == 0:
                    one, two = blocks[i], blocks[i + step]
                    blocks[i] = jnp.where(low, one, pltpu.roll(two, 16 * step, 1))
                    blocks[i + step] = jnp.where(
                        low, pltpu.roll(one, 128 - 16 * step, 1), two
                    )
        x_hi, x_lo = split(jnp.concatenate(blocks, axis=0))
        once = nn(x_hi, w_hi) + (nn(x_lo, w_hi) + nn(x_hi, w_lo))
        turned[c, 0] = once[:, :128]
        turned[c, 1] = once[:, 128:]
        base = 256 + c * (REST + REST)
        cos = consts[base : base + half, :]
        sin = consts[base + half : base + REST, :]
        second = consts[base + REST : base + 2 * REST, : 3 * REST].astype(bf16)
        real, imag = [], []
        for col in range(width):
            re = turned.at[c, 0][pl.ds(col, half, stride=width), :]
            im = turned.at[c, 1][pl.ds(col, half, stride=width), :]
            real.append(re * cos + im * sin)
            imag.append(im * cos - re * sin)
        z = jnp.concatenate(
            [jnp.concatenate(real, axis=1), jnp.concatenate(imag, axis=1)], axis=0
        )
        z_hi, z_lo = split(z)
        part = nn(second, jnp.concatenate([z_hi, z_lo, z_hi], axis=0))
        if c == 0:
            for col in range(width):
                out[col] = part[:, col * 128 : (col + 1) * 128]
        else:
            for col in range(width):
                out[col] += part[:, col * 128 : (col + 1) * 128]

    for copy, _ in first_copies:
        copy.wait_send()
    for _, copy, _ in last_copies:
        copy.wait_send()
    for copy in shape_sends + to_across + to_sibling + forward:
        copy.wait_send()


def with_kernel(modal_history, stress_modes):
    elems, modes = lax.axis_size("elem"), lax.axis_size("mode")
    steps = modal_history.shape[0] * elems
    width = stress_modes.shape[1] // modes
    table = jnp.asarray(tables(steps))
    hist = modal_history.reshape(16, 2, 16, 128)
    hbm = pl.BlockSpec(memory_space=pl.ANY)
    dma = pltpu.SemaphoreType.DMA
    result = pl.pallas_call(
        functools.partial(fused, elems, modes, width),
        out_shape=jax.ShapeDtypeStruct((width, REST, RADIX), f32),
        in_specs=[hbm] * 3,
        out_specs=pl.BlockSpec(memory_space=pltpu.VMEM),
        scratch_shapes=[
            pltpu.VMEM((modes, 2, 16, 16, 128), f32),
            pltpu.VMEM((2, modes, 256, 128), bf16),
            pltpu.VMEM((2, modes, 256, 128), bf16),
            pltpu.VMEM((modes * width, 128), f32),
            pltpu.VMEM((modes, 16, 128), f32),
            pltpu.VMEM((modes, 16, 128), f32),
            pltpu.VMEM((elems, modes * width, 128), f32),
            pltpu.VMEM((elems * 16, modes * 128), f32),
            pltpu.VMEM((elems, 2, 2 * width, 128), f32),
            pltpu.VMEM((elems, 2, 2 * width, 128), f32),
            pltpu.VMEM((2, 2, REST // 2 * width, 128), f32),
            pltpu.VMEM(table.shape, f32),
            dma((2,)), dma((2,)),
            dma((3, 2)), dma((3, 2)),
            dma((3,)), dma((3,)),
            dma((elems,)), dma((elems,)),
            dma((elems, 2)), dma((elems, 2)),
        ],
        compiler_params=pltpu.CompilerParams(
            collective_id=0, has_side_effects=True, vmem_limit_bytes=60 * 1024 * 1024
        ),
    )(hist, stress_modes.T, table)
    ordered = result.reshape(width, REST // 2, 2, RADIX).transpose(0, 2, 1, 3)
    return ordered.reshape(width, 2, REST // 2 * RADIX)


def per_device(modal_history, stress_modes):
    elems, modes = lax.axis_size("elem"), lax.axis_size("mode")
    fits = (
        elems == 8
        and modes == 4
        and modal_history.shape == (512, 128)
        and stress_modes.shape == (128, 48)
    )
    body = with_kernel if fits else plain
    return body(modal_history, stress_modes)


def solution(mesh):
    placed = (P("elem", "mode"), P("mode", "elem"))
    return jax.shard_map(
        per_device,
        mesh=mesh,
        in_specs=placed,
        out_specs=P(("elem", "mode"), None, None),
        check_vma=False,
    )
```

```python
import functools
import math

import jax
import jax.numpy as jnp
import ml_dtypes
import numpy as np
from jax import lax
from jax.experimental import pallas as pl
from jax.experimental.pallas import tpu as pltpu
from jax.sharding import PartitionSpec as P

highest = lax.Precision.HIGHEST
MESH = pl.DeviceIdType.MESH
f32, bf16 = jnp.float32, jnp.bfloat16

RADIX = 128
REST = 32


def spectra(signal):
    columns = signal.shape[0]
    radix = 64
    halved = radix // 2
    blocked = signal.reshape(columns, radix, radix)
    counter = jnp.arange(radix, dtype=jnp.int32)
    products = counter[:, None] * counter[None, :]
    small_angle = (products % radix).astype(jnp.float32) * (2.0 * math.pi / radix)
    cosine_small = jnp.cos(small_angle)
    sine_small = jnp.sin(small_angle)
    twist_angle = (products % (radix * radix)).astype(jnp.float32) * (
        2.0 * math.pi / (radix * radix)
    )
    twist_cos = jnp.cos(twist_angle)
    twist_sin = jnp.sin(twist_angle)
    first_real = jnp.einsum("cab,ak->cbk", blocked, cosine_small, precision=highest)
    first_imag = -jnp.einsum("cab,ak->cbk", blocked, sine_small, precision=highest)
    turned_real = first_real * twist_cos + first_imag * twist_sin
    turned_imag = first_imag * twist_cos - first_real * twist_sin
    cosine_half = cosine_small[:, :halved]
    sine_half = sine_small[:, :halved]
    final_real = jnp.einsum(
        "cbk,bj->cjk", turned_real, cosine_half, precision=highest
    ) + jnp.einsum("cbk,bj->cjk", turned_imag, sine_half, precision=highest)
    final_imag = jnp.einsum(
        "cbk,bj->cjk", turned_imag, cosine_half, precision=highest
    ) - jnp.einsum("cbk,bj->cjk", turned_real, sine_half, precision=highest)
    stacked = jnp.stack([final_real, final_imag], axis=1) * (1.0 / radix)
    return stacked.reshape(columns, 2, halved * radix)


def plain(modal_history, stress_modes):
    elem_count = lax.axis_size("elem")
    mode_count = lax.axis_size("mode")
    local_steps = modal_history.shape[0]
    partial_value = jnp.einsum(
        "mp,tm->pt",
        lax.all_gather(stress_modes, "elem", axis=1, tiled=True),
        modal_history,
        precision=highest,
        preferred_element_type=jnp.float32,
    )
    owned_width = partial_value.shape[0] // (elem_count * mode_count)
    reordered = partial_value.reshape(elem_count, mode_count, owned_width, local_steps)
    reordered = reordered.transpose(1, 0, 2, 3).reshape(
        mode_count * elem_count * owned_width, local_steps
    )
    summed = lax.psum_scatter(reordered, "mode", scatter_dimension=0, tiled=True)
    stress = lax.all_to_all(summed, "elem", split_axis=0, concat_axis=1, tiled=True)
    return spectra(stress)


def split_np(x):
    hi = x.astype(np.float32).astype(ml_dtypes.bfloat16)
    lo = (x - hi.astype(np.float64)).astype(np.float32).astype(ml_dtypes.bfloat16)
    return hi, lo


def tables(steps):
    two_pi = 2.0 * np.pi
    a = np.arange(RADIX)
    ang = two_pi * ((a[:, None] * a[None, :]) % RADIX) / RADIX
    parts = [np.cos(ang), -np.sin(ang)]
    k2 = np.arange(REST // 2)
    for c in range(2):
        row = np.arange(REST // 2)
        b = (2 * c + row % 2) * 8 + row // 2
        twist = two_pi * ((b[:, None] * a[None, :]) % steps) / steps
        parts += [np.cos(twist), np.sin(twist)]
        last = two_pi * ((k2[:, None] * b[None, :]) % REST) / REST
        real = np.concatenate([np.cos(last), np.sin(last)], axis=1)
        imag = np.concatenate([-np.sin(last), np.cos(last)], axis=1)
        second = np.stack([real, imag], axis=1).reshape(REST, REST) / math.sqrt(steps)
        hi, lo = (p.astype(np.float64) for p in split_np(second))
        parts.append(np.concatenate([hi, hi, lo, np.zeros_like(hi)], axis=1))
    return np.concatenate(parts, axis=0).astype(np.float32)


def split(x):
    hi = x.astype(bf16)
    lo = (x - hi.astype(f32)).astype(bf16)
    return hi, lo


def nt(a, b):
    return lax.dot_general(
        a, b, (((1,), (1,)), ((), ())), preferred_element_type=f32
    )


def nn(a, b):
    return jnp.dot(a, b, preferred_element_type=f32)


def fused(
    elems, modes, width,
    hist, shapes, table,
    out,
    hbuf, h_his, h_los, gathered, parts, other_parts, outbox, inbox,
    turned, consts,
    own_sem, fetch_sem, hs_sem, hr_sem, s1s_sem, s1r_sem, s2s_sem, s2r_sem,
    ps_sem, pr_sem, as_sem, ar_sem,
):
    chunks = 2
    e = lax.axis_index("elem")
    m = lax.axis_index("mode")
    x, core = m // 2, m % 2
    sibling = m + 1 - 2 * core
    across = (m + 2) % modes
    beside = e + 1 - 2 * (e % 2)
    halves = (x, 1 - x)

    fetch_shapes = pltpu.make_async_copy(
        shapes.at[x], gathered.at[e, x], fetch_sem.at[0]
    )
    fetch_table = pltpu.make_async_copy(table, consts, fetch_sem.at[1])
    own = [
        pltpu.make_async_copy(hist.at[:, c], hbuf.at[x, c], own_sem.at[c])
        for c in range(chunks)
    ]
    fetch_shapes.start()
    for copy in own:
        copy.start()
    fetch_table.start()

    barrier = pltpu.get_barrier_semaphore()
    for d in range(1, elems):
        pl.semaphore_signal(
            barrier, inc=1, device_id=((e + d) % elems, m), device_id_type=MESH
        )
    for peer in (across, sibling):
        pl.semaphore_signal(barrier, inc=1, device_id=(e, peer), device_id_type=MESH)
    pl.semaphore_wait(barrier, elems - 1 + 2)

    to_regroup = pltpu.make_async_remote_copy(
        shapes.at[1 - x], gathered.at[e, x], s1s_sem.at[0], s1r_sem.at[0],
        device_id=(e, across), device_id_type=MESH,
    )
    from_regroup = pltpu.make_async_remote_copy(
        shapes.at[1 - x], gathered.at[e, 1 - x], s1s_sem.at[0], s1r_sem.at[0],
        device_id=(e, across), device_id_type=MESH,
    )
    to_regroup.start()

    def shape_copy(slot, block, kind, peer):
        ref = gathered.at[block, halves[kind]]
        return pltpu.make_async_remote_copy(
            ref, ref, s2s_sem.at[slot, kind], s2r_sem.at[slot, kind],
            device_id=(peer, m), device_id_type=MESH,
        )

    shape_sends = []
    steps_z = [elems // 2] + [d for d in range(2, elems, 2) if d != elems // 2]

    def send_shapes(kind):
        for d in steps_z:
            shape_sends.append(shape_copy(d, e, kind, (e + d) % elems))
            shape_sends[-1].start()
        shape_sends.append(shape_copy(1, e, kind, beside))
        shape_sends[-1].start()

    fetch_shapes.wait()
    send_shapes(0)

    to_across, from_across = [
        [
            pltpu.make_async_remote_copy(
                hist.at[:, c], hbuf.at[origin, c], hs_sem.at[c], hr_sem.at[c],
                device_id=(e, across), device_id_type=MESH,
            )
            for c in range(chunks)
        ]
        for origin in (x, 1 - x)
    ]
    for copy in to_across:
        copy.start()

    def split_history(origin, c):
        flat = hbuf.at[origin, c].reshape(256, 128)
        turned_rows = [flat[pl.ds(i, 16, stride=16), :] for i in range(16)]
        hi, lo = split(jnp.concatenate(turned_rows, axis=0))
        h_his[c, origin] = hi
        h_los[c, origin] = lo

    from_regroup.wait_recv()
    send_shapes(1)
    for c in range(chunks):
        own[c].wait()
        split_history(x, c)

    for kind in range(2):
        for d in sorted(steps_z, key=lambda d: min(d, elems - d)):
            source = (e + elems - d) % elems
            shape_copy(d, source, kind, source).wait_recv()
            copy = shape_copy(d + 1, source, kind, beside)
            copy.start()
            shape_sends.append(copy)

    from_across[0].wait_recv()
    split_history(1 - x, 0)

    for kind in range(2):
        shape_copy(1, beside, kind, beside).wait_recv()
        for d in steps_z:
            source = (beside + elems - d) % elems
            shape_copy(d + 1, source, kind, beside).wait_recv()
    s_hi, s_lo = split(
        jnp.concatenate(
            [
                jnp.concatenate([gathered[owner, h] for h in range(2)], axis=1)
                for owner in range(elems)
            ],
            axis=0,
        )
    )
    s_both = jnp.concatenate([s_hi, s_lo], axis=0)
    rows = s_hi.shape[0]

    order = sorted(range(1, elems), key=lambda d: -min(d, elems - d))
    last_copies, part_copies = [], []
    for c in range(chunks):
        if c:
            from_across[c].wait_recv()
            split_history(1 - x, c)
        h_hi = jnp.concatenate([h_his[c, h] for h in range(2)], axis=1)
        h_lo = jnp.concatenate([h_los[c, h] for h in range(2)], axis=1)
        both = nt(s_both, h_hi)
        stress = both[:rows] + (both[rows:] + nt(s_hi, h_lo))
        for owner in range(elems):
            for k in range(2):
                for h in range(2):
                    start = (owner * 2 + k) * width
                    parts[c, k, owner, h * width : (h + 1) * width, :] = stress[
                        start : start + width, h * 128 : (h + 1) * 128
                    ]
        copy = pltpu.make_async_remote_copy(
            parts.at[c, 1 - core], other_parts.at[c], ps_sem.at[c], pr_sem.at[c],
            device_id=(e, sibling), device_id_type=MESH,
        )
        copy.start()
        part_copies.append(copy)
        copy.wait_recv()
        whole = parts[c, core] + other_parts[c]
        outbox[c] = whole
        for d in order:
            peer, source = (e + d) % elems, (e + elems - d) % elems
            copy = pltpu.make_async_remote_copy(
                outbox.at[c, peer], inbox.at[c, e], as_sem.at[d, c], ar_sem.at[d, c],
                device_id=(peer, m), device_id_type=MESH,
            )
            landed = pltpu.make_async_remote_copy(
                outbox.at[c, peer], inbox.at[c, source], as_sem.at[d, c],
                ar_sem.at[d, c], device_id=(peer, m), device_id_type=MESH,
            )
            copy.start()
            last_copies.append((c, copy, landed))
        inbox[c, e] = outbox[c, e]

    fetch_table.wait()
    w_hi, w_lo = split(
        jnp.concatenate([consts[:128, :], consts[128:256, :]], axis=1)
    )
    half = REST // 2
    total = None
    for c in range(chunks):
        for chunk, _, landed in last_copies:
            if chunk == c:
                landed.wait_recv()
        blocks = [inbox[c, i] for i in range(elems)]
        group = lax.broadcasted_iota(jnp.int32, blocks[0].shape, 1) // 16
        for step in (4, 2, 1):
            low = (group // step) % 2 == 0
            for i in range(elems):
                if (i // step) % 2 == 0:
                    one, two = blocks[i], blocks[i + step]
                    blocks[i] = jnp.where(low, one, pltpu.roll(two, 16 * step, 1))
                    blocks[i + step] = jnp.where(
                        low, pltpu.roll(one, 128 - 16 * step, 1), two
                    )
        x_hi, x_lo = split(jnp.concatenate(blocks, axis=0))
        once = nn(x_hi, w_hi) + (nn(x_lo, w_hi) + nn(x_hi, w_lo))
        turned[c, 0] = once[:, :128]
        turned[c, 1] = once[:, 128:]
        base = 256 + c * (REST + REST)
        cos = consts[base : base + half, :]
        sin = consts[base + half : base + REST, :]
        second = consts[base + REST : base + 2 * REST, : 3 * REST].astype(bf16)
        real, imag = [], []
        for col in range(width):
            re = turned.at[c, 0][pl.ds(col, half, stride=width), :]
            im = turned.at[c, 1][pl.ds(col, half, stride=width), :]
            real.append(re * cos + im * sin)
            imag.append(im * cos - re * sin)
        z = jnp.concatenate(
            [jnp.concatenate(real, axis=1), jnp.concatenate(imag, axis=1)], axis=0
        )
        z_hi, z_lo = split(z)
        part = nn(second, jnp.concatenate([z_hi, z_lo, z_hi], axis=0))
        if c == 0:
            for col in range(width):
                out[col] = part[:, col * 128 : (col + 1) * 128]
        else:
            for col in range(width):
                out[col] += part[:, col * 128 : (col + 1) * 128]

    for _, copy, _ in last_copies:
        copy.wait_send()
    for copy in [to_regroup] + shape_sends + to_across + part_copies:
        copy.wait_send()


def with_kernel(modal_history, stress_modes):
    elems, modes = lax.axis_size("elem"), lax.axis_size("mode")
    steps = modal_history.shape[0] * elems
    width = stress_modes.shape[1] // modes
    table = jnp.asarray(tables(steps))
    hist = modal_history.reshape(16, 2, 16, 128)
    shapes = stress_modes.T.reshape(2, 2 * width, 128)
    hbm = pl.BlockSpec(memory_space=pl.ANY)
    dma = pltpu.SemaphoreType.DMA
    result = pl.pallas_call(
        functools.partial(fused, elems, modes, width),
        out_shape=jax.ShapeDtypeStruct((width, REST, RADIX), f32),
        in_specs=[hbm] * 3,
        out_specs=pl.BlockSpec(memory_space=pltpu.VMEM),
        scratch_shapes=[
            pltpu.VMEM((2, 2, 16, 16, 128), f32),
            pltpu.VMEM((2, 2, 256, 128), bf16),
            pltpu.VMEM((2, 2, 256, 128), bf16),
            pltpu.VMEM((elems, 2, 2 * width, 128), f32),
            pltpu.VMEM((2, 2, elems, 2 * width, 128), f32),
            pltpu.VMEM((2, elems, 2 * width, 128), f32),
            pltpu.VMEM((2, elems, 2 * width, 128), f32),
            pltpu.VMEM((2, elems, 2 * width, 128), f32),
            pltpu.VMEM((2, 2, REST // 2 * width, 128), f32),
            pltpu.VMEM(table.shape, f32),
            dma((2,)), dma((2,)),
            dma((2,)), dma((2,)),
            dma((1,)), dma((1,)),
            dma((elems, 2)), dma((elems, 2)),
            dma((2,)), dma((2,)),
            dma((elems, 2)), dma((elems, 2)),
        ],
        compiler_params=pltpu.CompilerParams(
            collective_id=0, has_side_effects=True, vmem_limit_bytes=55000 * 1024
        ),
    )(hist, shapes, table)
    ordered = result.reshape(width, REST // 2, 2, RADIX).transpose(0, 2, 1, 3)
    return ordered.reshape(width, 2, REST // 2 * RADIX)


def per_device(modal_history, stress_modes):
    elems, modes = lax.axis_size("elem"), lax.axis_size("mode")
    fits = (
        elems == 8
        and modes == 4
        and modal_history.shape == (512, 128)
        and stress_modes.shape == (128, 48)
    )
    body = with_kernel if fits else plain
    return body(modal_history, stress_modes)


def solution(mesh):
    placed = (P("elem", "mode"), P("mode", "elem"))
    return jax.shard_map(
        per_device,
        mesh=mesh,
        in_specs=placed,
        out_specs=P(("elem", "mode"), None, None),
        check_vma=False,
    )
```

```python
import functools
import math

import jax
import jax.numpy as jnp
import ml_dtypes
import numpy as np
from jax import lax
from jax.experimental import pallas as pl
from jax.experimental.pallas import tpu as pltpu
from jax.sharding import PartitionSpec as P

highest = lax.Precision.HIGHEST
MESH = pl.DeviceIdType.MESH
f32, bf16 = jnp.float32, jnp.bfloat16

RADIX = 128
REST = 32


def spectra(signal):
    columns = signal.shape[0]
    radix = 64
    halved = radix // 2
    blocked = signal.reshape(columns, radix, radix)
    counter = jnp.arange(radix, dtype=jnp.int32)
    products = counter[:, None] * counter[None, :]
    small_angle = (products % radix).astype(jnp.float32) * (2.0 * math.pi / radix)
    cosine_small = jnp.cos(small_angle)
    sine_small = jnp.sin(small_angle)
    twist_angle = (products % (radix * radix)).astype(jnp.float32) * (
        2.0 * math.pi / (radix * radix)
    )
    twist_cos = jnp.cos(twist_angle)
    twist_sin = jnp.sin(twist_angle)
    first_real = jnp.einsum("cab,ak->cbk", blocked, cosine_small, precision=highest)
    first_imag = -jnp.einsum("cab,ak->cbk", blocked, sine_small, precision=highest)
    turned_real = first_real * twist_cos + first_imag * twist_sin
    turned_imag = first_imag * twist_cos - first_real * twist_sin
    cosine_half = cosine_small[:, :halved]
    sine_half = sine_small[:, :halved]
    final_real = jnp.einsum(
        "cbk,bj->cjk", turned_real, cosine_half, precision=highest
    ) + jnp.einsum("cbk,bj->cjk", turned_imag, sine_half, precision=highest)
    final_imag = jnp.einsum(
        "cbk,bj->cjk", turned_imag, cosine_half, precision=highest
    ) - jnp.einsum("cbk,bj->cjk", turned_real, sine_half, precision=highest)
    stacked = jnp.stack([final_real, final_imag], axis=1) * (1.0 / radix)
    return stacked.reshape(columns, 2, halved * radix)


def plain(modal_history, stress_modes):
    elem_count = lax.axis_size("elem")
    mode_count = lax.axis_size("mode")
    local_steps = modal_history.shape[0]
    partial_value = jnp.einsum(
        "mp,tm->pt",
        lax.all_gather(stress_modes, "elem", axis=1, tiled=True),
        modal_history,
        precision=highest,
        preferred_element_type=jnp.float32,
    )
    owned_width = partial_value.shape[0] // (elem_count * mode_count)
    reordered = partial_value.reshape(elem_count, mode_count, owned_width, local_steps)
    reordered = reordered.transpose(1, 0, 2, 3).reshape(
        mode_count * elem_count * owned_width, local_steps
    )
    summed = lax.psum_scatter(reordered, "mode", scatter_dimension=0, tiled=True)
    stress = lax.all_to_all(summed, "elem", split_axis=0, concat_axis=1, tiled=True)
    return spectra(stress)


def split_np(x):
    hi = x.astype(np.float32).astype(ml_dtypes.bfloat16)
    lo = (x - hi.astype(np.float64)).astype(np.float32).astype(ml_dtypes.bfloat16)
    return hi, lo


def tables(steps):
    two_pi = 2.0 * np.pi
    a = np.arange(RADIX)
    ang = two_pi * ((a[:, None] * a[None, :]) % RADIX) / RADIX
    parts = [np.cos(ang), -np.sin(ang)]
    k2 = np.arange(REST // 2)
    for c in range(2):
        row = np.arange(REST // 2)
        b = (2 * c + row % 2) * 8 + row // 2
        twist = two_pi * ((b[:, None] * a[None, :]) % steps) / steps
        parts += [np.cos(twist), np.sin(twist)]
        last = two_pi * ((k2[:, None] * b[None, :]) % REST) / REST
        real = np.concatenate([np.cos(last), np.sin(last)], axis=1)
        imag = np.concatenate([-np.sin(last), np.cos(last)], axis=1)
        second = np.stack([real, imag], axis=1).reshape(REST, REST) / math.sqrt(steps)
        hi, lo = (p.astype(np.float64) for p in split_np(second))
        parts.append(np.concatenate([hi, hi, lo, np.zeros_like(hi)], axis=1))
    return np.concatenate(parts, axis=0).astype(np.float32)


def split(x):
    hi = x.astype(bf16)
    lo = (x - hi.astype(f32)).astype(bf16)
    return hi, lo


def nt(a, b):
    return lax.dot_general(
        a, b, (((1,), (1,)), ((), ())), preferred_element_type=f32
    )


def nn(a, b):
    return jnp.dot(a, b, preferred_element_type=f32)


def fused(
    elems, modes, width,
    hist, shapes, table,
    out,
    hbuf, h_his, h_los, gathered, parts, other_parts, outbox, inbox,
    turned, consts,
    own_sem, fetch_sem, hs_sem, hr_sem, s1s_sem, s1r_sem, z_send, z_recv, y_send, y_recv,
    ps_sem, pr_sem, as_sem, ar_sem,
):
    chunks = 2
    e = lax.axis_index("elem")
    m = lax.axis_index("mode")
    x, core = m // 2, m % 2
    sibling = m + 1 - 2 * core
    across = (m + 2) % modes
    beside = e + 1 - 2 * (e % 2)
    halves = (x, 1 - x)
    z, top = e // 2, elems // 2 - 1

    fetch_shapes = pltpu.make_async_copy(
        shapes.at[x], gathered.at[e, x], fetch_sem.at[0]
    )
    fetch_table = pltpu.make_async_copy(table, consts, fetch_sem.at[1])
    own = [
        pltpu.make_async_copy(hist.at[:, c], hbuf.at[x, c], own_sem.at[c])
        for c in range(chunks)
    ]
    fetch_shapes.start()
    for copy in own:
        copy.start()
    fetch_table.start()

    below, above = z > 0, z < top
    barrier = pltpu.get_barrier_semaphore()

    def greet(device):
        pl.semaphore_signal(barrier, inc=1, device_id=device, device_id_type=MESH)

    greet((e, across))
    greet((e, sibling))
    greet((beside, m))

    @pl.when(below)
    def _():
        greet((e - 2, m))

    @pl.when(above)
    def _():
        greet((e + 2, m))

    at_end = (z == 0).astype(jnp.int32) + (z == top).astype(jnp.int32)
    pl.semaphore_wait(barrier, 5 - at_end)

    to_regroup = pltpu.make_async_remote_copy(
        shapes.at[1 - x], gathered.at[e, x], s1s_sem.at[0], s1r_sem.at[0],
        device_id=(e, across), device_id_type=MESH,
    )
    from_regroup = pltpu.make_async_remote_copy(
        shapes.at[1 - x], gathered.at[e, 1 - x], s1s_sem.at[0], s1r_sem.at[0],
        device_id=(e, across), device_id_type=MESH,
    )
    to_regroup.start()

    def along(way, distance, kind, block, peer):
        ref = gathered.at[block, halves[kind]]
        return pltpu.make_async_remote_copy(
            ref, ref, z_send.at[way, distance, kind], z_recv.at[way, distance, kind],
            device_id=(peer, m), device_id_type=MESH,
        )

    def aside(level, kind, block):
        ref = gathered.at[block, halves[kind]]
        return pltpu.make_async_remote_copy(
            ref, ref, y_send.at[level, kind], y_recv.at[level, kind],
            device_id=(beside, m), device_id_type=MESH,
        )

    def pass_on(way, distance, kind, act):
        if way == 0:
            @pl.when(above & (z >= distance))
            def _():
                act(along(0, distance, kind, e - 2 * distance, e + 2))
        else:
            @pl.when(below & (z + distance <= top))
            def _():
                act(along(1, distance, kind, e + 2 * distance, e - 2))

    def send_shapes(kind):
        for way in range(2):
            pass_on(way, 0, kind, lambda copy: copy.start())
        aside(z, kind, e).start()

    def relay(distance, kind):
        @pl.when(z >= distance)
        def _():
            block = e - 2 * distance
            along(0, distance - 1, kind, block, e - 2).wait_recv()
            if distance < top:
                pass_on(0, distance, kind, lambda copy: copy.start())
            aside(z - distance, kind, block).start()

        @pl.when(z + distance <= top)
        def _():
            block = e + 2 * distance
            along(1, distance - 1, kind, block, e + 2).wait_recv()
            if distance < top:
                pass_on(1, distance, kind, lambda copy: copy.start())
            aside(z + distance, kind, block).start()

    fetch_shapes.wait()
    send_shapes(0)

    to_across, from_across = [
        [
            pltpu.make_async_remote_copy(
                hist.at[:, c], hbuf.at[origin, c], hs_sem.at[c], hr_sem.at[c],
                device_id=(e, across), device_id_type=MESH,
            )
            for c in range(chunks)
        ]
        for origin in (x, 1 - x)
    ]
    for copy in to_across:
        copy.start()

    def split_history(origin, c):
        flat = hbuf.at[origin, c].reshape(256, 128)
        turned_rows = [flat[pl.ds(i, 16, stride=16), :] for i in range(16)]
        hi, lo = split(jnp.concatenate(turned_rows, axis=0))
        h_his[c, origin] = hi
        h_los[c, origin] = lo

    from_regroup.wait_recv()
    send_shapes(1)
    for c in range(chunks):
        own[c].wait()
        split_history(x, c)

    for distance in range(1, top + 1):
        for kind in range(2):
            relay(distance, kind)

    from_across[0].wait_recv()
    split_history(1 - x, 0)

    for kind in range(2):
        for level in range(top + 1):
            aside(level, kind, 2 * level + beside % 2).wait_recv()
    s_hi, s_lo = split(
        jnp.concatenate(
            [
                jnp.concatenate([gathered[owner, h] for h in range(2)], axis=1)
                for owner in range(elems)
            ],
            axis=0,
        )
    )
    s_both = jnp.concatenate([s_hi, s_lo], axis=0)
    rows = s_hi.shape[0]

    order = sorted(range(1, elems), key=lambda d: -min(d, elems - d))
    last_copies, part_copies = [], []
    for c in range(chunks):
        if c:
            from_across[c].wait_recv()
            split_history(1 - x, c)
        h_hi = jnp.concatenate([h_his[c, h] for h in range(2)], axis=1)
        h_lo = jnp.concatenate([h_los[c, h] for h in range(2)], axis=1)
        both = nt(s_both, h_hi)
        stress = both[:rows] + (both[rows:] + nt(s_hi, h_lo))
        for owner in range(elems):
            for k in range(2):
                for h in range(2):
                    start = (owner * 2 + k) * width
                    parts[c, k, owner, h * width : (h + 1) * width, :] = stress[
                        start : start + width, h * 128 : (h + 1) * 128
                    ]
        copy = pltpu.make_async_remote_copy(
            parts.at[c, 1 - core], other_parts.at[c], ps_sem.at[c], pr_sem.at[c],
            device_id=(e, sibling), device_id_type=MESH,
        )
        copy.start()
        part_copies.append(copy)
        copy.wait_recv()
        whole = parts[c, core] + other_parts[c]
        outbox[c] = whole
        for d in order:
            peer, source = (e + d) % elems, (e + elems - d) % elems
            copy = pltpu.make_async_remote_copy(
                outbox.at[c, peer], inbox.at[c, e], as_sem.at[d, c], ar_sem.at[d, c],
                device_id=(peer, m), device_id_type=MESH,
            )
            landed = pltpu.make_async_remote_copy(
                outbox.at[c, peer], inbox.at[c, source], as_sem.at[d, c],
                ar_sem.at[d, c], device_id=(peer, m), device_id_type=MESH,
            )
            copy.start()
            last_copies.append((c, copy, landed))
        inbox[c, e] = outbox[c, e]

    fetch_table.wait()
    w_hi, w_lo = split(
        jnp.concatenate([consts[:128, :], consts[128:256, :]], axis=1)
    )
    half = REST // 2
    total = None
    for c in range(chunks):
        for chunk, _, landed in last_copies:
            if chunk == c:
                landed.wait_recv()
        blocks = [inbox[c, i] for i in range(elems)]
        group = lax.broadcasted_iota(jnp.int32, blocks[0].shape, 1) // 16
        for step in (4, 2, 1):
            low = (group // step) % 2 == 0
            for i in range(elems):
                if (i // step) % 2 == 0:
                    one, two = blocks[i], blocks[i + step]
                    blocks[i] = jnp.where(low, one, pltpu.roll(two, 16 * step, 1))
                    blocks[i + step] = jnp.where(
                        low, pltpu.roll(one, 128 - 16 * step, 1), two
                    )
        x_hi, x_lo = split(jnp.concatenate(blocks, axis=0))
        once = nn(x_hi, w_hi) + (nn(x_lo, w_hi) + nn(x_hi, w_lo))
        turned[c, 0] = once[:, :128]
        turned[c, 1] = once[:, 128:]
        base = 256 + c * (REST + REST)
        cos = consts[base : base + half, :]
        sin = consts[base + half : base + REST, :]
        second = consts[base + REST : base + 2 * REST, : 3 * REST].astype(bf16)
        real, imag = [], []
        for col in range(width):
            re = turned.at[c, 0][pl.ds(col, half, stride=width), :]
            im = turned.at[c, 1][pl.ds(col, half, stride=width), :]
            real.append(re * cos + im * sin)
            imag.append(im * cos - re * sin)
        waves = jnp.concatenate(
            [jnp.concatenate(real, axis=1), jnp.concatenate(imag, axis=1)], axis=0
        )
        z_hi, z_lo = split(waves)
        part = nn(second, jnp.concatenate([z_hi, z_lo, z_hi], axis=0))
        if c == 0:
            for col in range(width):
                out[col] = part[:, col * 128 : (col + 1) * 128]
        else:
            for col in range(width):
                out[col] += part[:, col * 128 : (col + 1) * 128]

    for _, copy, _ in last_copies:
        copy.wait_send()
    for copy in [to_regroup] + to_across + part_copies:
        copy.wait_send()
    for kind in range(2):
        for distance in range(top):
            for way in range(2):
                pass_on(way, distance, kind, lambda copy: copy.wait_send())
        for level in range(top + 1):
            aside(level, kind, 2 * level + e % 2).wait_send()


def with_kernel(modal_history, stress_modes):
    elems, modes = lax.axis_size("elem"), lax.axis_size("mode")
    steps = modal_history.shape[0] * elems
    width = stress_modes.shape[1] // modes
    table = jnp.asarray(tables(steps))
    hist = modal_history.reshape(16, 2, 16, 128)
    shapes = stress_modes.T.reshape(2, 2 * width, 128)
    hbm = pl.BlockSpec(memory_space=pl.ANY)
    dma = pltpu.SemaphoreType.DMA
    result = pl.pallas_call(
        functools.partial(fused, elems, modes, width),
        out_shape=jax.ShapeDtypeStruct((width, REST, RADIX), f32),
        in_specs=[hbm] * 3,
        out_specs=pl.BlockSpec(memory_space=pltpu.VMEM),
        scratch_shapes=[
            pltpu.VMEM((2, 2, 16, 16, 128), f32),
            pltpu.VMEM((2, 2, 256, 128), bf16),
            pltpu.VMEM((2, 2, 256, 128), bf16),
            pltpu.VMEM((elems, 2, 2 * width, 128), f32),
            pltpu.VMEM((2, 2, elems, 2 * width, 128), f32),
            pltpu.VMEM((2, elems, 2 * width, 128), f32),
            pltpu.VMEM((2, elems, 2 * width, 128), f32),
            pltpu.VMEM((2, elems, 2 * width, 128), f32),
            pltpu.VMEM((2, 2, REST // 2 * width, 128), f32),
            pltpu.VMEM(table.shape, f32),
            dma((2,)), dma((2,)),
            dma((2,)), dma((2,)),
            dma((1,)), dma((1,)),
            dma((2, 3, 2)), dma((2, 3, 2)),
            dma((elems // 2, 2)), dma((elems // 2, 2)),
            dma((2,)), dma((2,)),
            dma((elems, 2)), dma((elems, 2)),
        ],
        compiler_params=pltpu.CompilerParams(
            collective_id=0, has_side_effects=True, vmem_limit_bytes=55000 * 1024
        ),
    )(hist, shapes, table)
    ordered = result.reshape(width, REST // 2, 2, RADIX).transpose(0, 2, 1, 3)
    return ordered.reshape(width, 2, REST // 2 * RADIX)


def per_device(modal_history, stress_modes):
    elems, modes = lax.axis_size("elem"), lax.axis_size("mode")
    fits = (
        elems == 8
        and modes == 4
        and modal_history.shape == (512, 128)
        and stress_modes.shape == (128, 48)
    )
    body = with_kernel if fits else plain
    return body(modal_history, stress_modes)


def solution(mesh):
    placed = (P("elem", "mode"), P("mode", "elem"))
    return jax.shard_map(
        per_device,
        mesh=mesh,
        in_specs=placed,
        out_specs=P(("elem", "mode"), None, None),
        check_vma=False,
    )
```

```python
import functools
import math

import jax
import jax.numpy as jnp
import ml_dtypes
import numpy as np
from jax import lax
from jax.experimental import pallas as pl
from jax.experimental.pallas import tpu as pltpu
from jax.sharding import PartitionSpec as P

highest = lax.Precision.HIGHEST
MESH = pl.DeviceIdType.MESH
f32, bf16 = jnp.float32, jnp.bfloat16

RADIX = 128
REST = 32


def spectra(signal):
    columns = signal.shape[0]
    radix = 64
    halved = radix // 2
    blocked = signal.reshape(columns, radix, radix)
    counter = jnp.arange(radix, dtype=jnp.int32)
    products = counter[:, None] * counter[None, :]
    small_angle = (products % radix).astype(jnp.float32) * (2.0 * math.pi / radix)
    cosine_small = jnp.cos(small_angle)
    sine_small = jnp.sin(small_angle)
    twist_angle = (products % (radix * radix)).astype(jnp.float32) * (
        2.0 * math.pi / (radix * radix)
    )
    twist_cos = jnp.cos(twist_angle)
    twist_sin = jnp.sin(twist_angle)
    first_real = jnp.einsum("cab,ak->cbk", blocked, cosine_small, precision=highest)
    first_imag = -jnp.einsum("cab,ak->cbk", blocked, sine_small, precision=highest)
    turned_real = first_real * twist_cos + first_imag * twist_sin
    turned_imag = first_imag * twist_cos - first_real * twist_sin
    cosine_half = cosine_small[:, :halved]
    sine_half = sine_small[:, :halved]
    final_real = jnp.einsum(
        "cbk,bj->cjk", turned_real, cosine_half, precision=highest
    ) + jnp.einsum("cbk,bj->cjk", turned_imag, sine_half, precision=highest)
    final_imag = jnp.einsum(
        "cbk,bj->cjk", turned_imag, cosine_half, precision=highest
    ) - jnp.einsum("cbk,bj->cjk", turned_real, sine_half, precision=highest)
    stacked = jnp.stack([final_real, final_imag], axis=1) * (1.0 / radix)
    return stacked.reshape(columns, 2, halved * radix)


def plain(modal_history, stress_modes):
    elem_count = lax.axis_size("elem")
    mode_count = lax.axis_size("mode")
    local_steps = modal_history.shape[0]
    partial_value = jnp.einsum(
        "mp,tm->pt",
        lax.all_gather(stress_modes, "elem", axis=1, tiled=True),
        modal_history,
        precision=highest,
        preferred_element_type=jnp.float32,
    )
    owned_width = partial_value.shape[0] // (elem_count * mode_count)
    reordered = partial_value.reshape(elem_count, mode_count, owned_width, local_steps)
    reordered = reordered.transpose(1, 0, 2, 3).reshape(
        mode_count * elem_count * owned_width, local_steps
    )
    summed = lax.psum_scatter(reordered, "mode", scatter_dimension=0, tiled=True)
    stress = lax.all_to_all(summed, "elem", split_axis=0, concat_axis=1, tiled=True)
    return spectra(stress)


def split_np(x):
    hi = x.astype(np.float32).astype(ml_dtypes.bfloat16)
    lo = (x - hi.astype(np.float64)).astype(np.float32).astype(ml_dtypes.bfloat16)
    return hi, lo


def tables(steps):
    two_pi = 2.0 * np.pi
    a = np.arange(RADIX)
    ang = two_pi * ((a[:, None] * a[None, :]) % RADIX) / RADIX
    parts = [np.cos(ang), -np.sin(ang)]
    k2 = np.arange(REST // 2)
    for c in range(2):
        row = np.arange(REST // 2)
        b = (2 * c + row % 2) * 8 + row // 2
        twist = two_pi * ((b[:, None] * a[None, :]) % steps) / steps
        parts += [np.cos(twist), np.sin(twist)]
        last = two_pi * ((k2[:, None] * b[None, :]) % REST) / REST
        real = np.concatenate([np.cos(last), np.sin(last)], axis=1)
        imag = np.concatenate([-np.sin(last), np.cos(last)], axis=1)
        second = np.stack([real, imag], axis=1).reshape(REST, REST) / math.sqrt(steps)
        hi, lo = (p.astype(np.float64) for p in split_np(second))
        parts.append(np.concatenate([hi, hi, lo, np.zeros_like(hi)], axis=1))
    return np.concatenate(parts, axis=0).astype(np.float32)


def split(x):
    hi = x.astype(bf16)
    lo = (x - hi.astype(f32)).astype(bf16)
    return hi, lo


def nt(a, b):
    return lax.dot_general(
        a, b, (((1,), (1,)), ((), ())), preferred_element_type=f32
    )


def nn(a, b):
    return jnp.dot(a, b, preferred_element_type=f32)


def fused(
    elems, modes, width,
    hist, shapes, table,
    out,
    hbuf, h_his, h_los, gathered, parts, other_parts, outbox, inbox,
    turned, consts,
    own_sem, fetch_sem, hs_sem, hr_sem, s1s_sem, s1r_sem, s2s_sem, s2r_sem,
    ps_sem, pr_sem, as_sem, ar_sem,
):
    chunks = 2
    e = lax.axis_index("elem")
    m = lax.axis_index("mode")
    x, core = m // 2, m % 2
    sibling = m + 1 - 2 * core
    across = (m + 2) % modes
    beside = e + 1 - 2 * (e % 2)
    halves = (x, 1 - x)

    fetch_shapes = pltpu.make_async_copy(
        shapes.at[x], gathered.at[e, x], fetch_sem.at[0]
    )
    fetch_table = pltpu.make_async_copy(table, consts, fetch_sem.at[1])
    own = [
        pltpu.make_async_copy(hist.at[:, c], hbuf.at[x, c], own_sem.at[c])
        for c in range(chunks)
    ]
    fetch_shapes.start()
    for copy in own:
        copy.start()
    fetch_table.start()

    barrier = pltpu.get_barrier_semaphore()
    for d in range(1, elems):
        pl.semaphore_signal(
            barrier, inc=1, device_id=((e + d) % elems, m), device_id_type=MESH
        )
    for peer in (across, sibling):
        pl.semaphore_signal(barrier, inc=1, device_id=(e, peer), device_id_type=MESH)
    pl.semaphore_wait(barrier, elems - 1 + 2)

    to_regroup = pltpu.make_async_remote_copy(
        shapes.at[1 - x], gathered.at[e, x], s1s_sem.at[0], s1r_sem.at[0],
        device_id=(e, across), device_id_type=MESH,
    )
    from_regroup = pltpu.make_async_remote_copy(
        shapes.at[1 - x], gathered.at[e, 1 - x], s1s_sem.at[0], s1r_sem.at[0],
        device_id=(e, across), device_id_type=MESH,
    )
    to_regroup.start()

    def shape_copy(slot, block, kind, peer):
        ref = gathered.at[block, halves[kind]]
        return pltpu.make_async_remote_copy(
            ref, ref, s2s_sem.at[slot, kind], s2r_sem.at[slot, kind],
            device_id=(peer, m), device_id_type=MESH,
        )

    shape_sends = []
    order = sorted(range(1, elems), key=lambda d: -min(d, elems - d))

    def send_shapes(kind):
        for d in order:
            shape_sends.append(shape_copy(d, e, kind, (e + d) % elems))
            shape_sends[-1].start()

    fetch_shapes.wait()
    send_shapes(0)

    to_across, from_across = [
        [
            pltpu.make_async_remote_copy(
                hist.at[:, c], hbuf.at[origin, c], hs_sem.at[c], hr_sem.at[c],
                device_id=(e, across), device_id_type=MESH,
            )
            for c in range(chunks)
        ]
        for origin in (x, 1 - x)
    ]
    for copy in to_across:
        copy.start()

    def split_history(origin, c):
        flat = hbuf.at[origin, c].reshape(256, 128)
        turned_rows = [flat[pl.ds(i, 16, stride=16), :] for i in range(16)]
        hi, lo = split(jnp.concatenate(turned_rows, axis=0))
        h_his[c, origin] = hi
        h_los[c, origin] = lo

    from_regroup.wait_recv()
    send_shapes(1)
    for c in range(chunks):
        own[c].wait()
        split_history(x, c)

    for c in range(chunks):
        from_across[c].wait_recv()
        split_history(1 - x, c)

    for kind in range(2):
        for d in order:
            source = (e + elems - d) % elems
            shape_copy(d, source, kind, source).wait_recv()
    s_hi, s_lo = split(
        jnp.concatenate(
            [
                jnp.concatenate([gathered[owner, h] for h in range(2)], axis=1)
                for owner in range(elems)
            ],
            axis=0,
        )
    )
    s_both = jnp.concatenate([s_hi, s_lo], axis=0)
    rows = s_hi.shape[0]

    last_copies, part_copies = [], []
    for c in range(chunks):
        h_hi = jnp.concatenate([h_his[c, h] for h in range(2)], axis=1)
        h_lo = jnp.concatenate([h_los[c, h] for h in range(2)], axis=1)
        both = nt(s_both, h_hi)
        stress = both[:rows] + (both[rows:] + nt(s_hi, h_lo))
        for owner in range(elems):
            for k in range(2):
                for h in range(2):
                    start = (owner * 2 + k) * width
                    parts[c, k, owner, h * width : (h + 1) * width, :] = stress[
                        start : start + width, h * 128 : (h + 1) * 128
                    ]
        copy = pltpu.make_async_remote_copy(
            parts.at[c, 1 - core], other_parts.at[c], ps_sem.at[c], pr_sem.at[c],
            device_id=(e, sibling), device_id_type=MESH,
        )
        copy.start()
        part_copies.append(copy)
    for c in range(chunks):
        part_copies[c].wait_recv()
        whole = parts[c, core] + other_parts[c]
        outbox[c] = whole
        for d in order:
            peer, source = (e + d) % elems, (e + elems - d) % elems
            copy = pltpu.make_async_remote_copy(
                outbox.at[c, peer], inbox.at[c, e], as_sem.at[d, c], ar_sem.at[d, c],
                device_id=(peer, m), device_id_type=MESH,
            )
            landed = pltpu.make_async_remote_copy(
                outbox.at[c, peer], inbox.at[c, source], as_sem.at[d, c],
                ar_sem.at[d, c], device_id=(peer, m), device_id_type=MESH,
            )
            copy.start()
            last_copies.append((c, copy, landed))
        inbox[c, e] = outbox[c, e]

    fetch_table.wait()
    w_hi, w_lo = split(
        jnp.concatenate([consts[:128, :], consts[128:256, :]], axis=1)
    )
    half = REST // 2
    total = None
    for c in range(chunks):
        for chunk, _, landed in last_copies:
            if chunk == c:
                landed.wait_recv()
        blocks = [inbox[c, i] for i in range(elems)]
        group = lax.broadcasted_iota(jnp.int32, blocks[0].shape, 1) // 16
        for step in (4, 2, 1):
            low = (group // step) % 2 == 0
            for i in range(elems):
                if (i // step) % 2 == 0:
                    one, two = blocks[i], blocks[i + step]
                    blocks[i] = jnp.where(low, one, pltpu.roll(two, 16 * step, 1))
                    blocks[i + step] = jnp.where(
                        low, pltpu.roll(one, 128 - 16 * step, 1), two
                    )
        x_hi, x_lo = split(jnp.concatenate(blocks, axis=0))
        once = nn(x_hi, w_hi) + (nn(x_lo, w_hi) + nn(x_hi, w_lo))
        turned[c, 0] = once[:, :128]
        turned[c, 1] = once[:, 128:]
        base = 256 + c * (REST + REST)
        cos = consts[base : base + half, :]
        sin = consts[base + half : base + REST, :]
        second = consts[base + REST : base + 2 * REST, : 3 * REST].astype(bf16)
        real, imag = [], []
        for col in range(width):
            re = turned.at[c, 0][pl.ds(col, half, stride=width), :]
            im = turned.at[c, 1][pl.ds(col, half, stride=width), :]
            real.append(re * cos + im * sin)
            imag.append(im * cos - re * sin)
        z = jnp.concatenate(
            [jnp.concatenate(real, axis=1), jnp.concatenate(imag, axis=1)], axis=0
        )
        z_hi, z_lo = split(z)
        part = nn(second, jnp.concatenate([z_hi, z_lo, z_hi], axis=0))
        if c == 0:
            for col in range(width):
                out[col] = part[:, col * 128 : (col + 1) * 128]
        else:
            for col in range(width):
                out[col] += part[:, col * 128 : (col + 1) * 128]

    for _, copy, _ in last_copies:
        copy.wait_send()
    for copy in [to_regroup] + shape_sends + to_across + part_copies:
        copy.wait_send()


def with_kernel(modal_history, stress_modes):
    elems, modes = lax.axis_size("elem"), lax.axis_size("mode")
    steps = modal_history.shape[0] * elems
    width = stress_modes.shape[1] // modes
    table = jnp.asarray(tables(steps))
    hist = modal_history.reshape(16, 2, 16, 128)
    shapes = stress_modes.T.reshape(2, 2 * width, 128)
    hbm = pl.BlockSpec(memory_space=pl.ANY)
    dma = pltpu.SemaphoreType.DMA
    result = pl.pallas_call(
        functools.partial(fused, elems, modes, width),
        out_shape=jax.ShapeDtypeStruct((width, REST, RADIX), f32),
        in_specs=[hbm] * 3,
        out_specs=pl.BlockSpec(memory_space=pltpu.VMEM),
        scratch_shapes=[
            pltpu.VMEM((2, 2, 16, 16, 128), f32),
            pltpu.VMEM((2, 2, 256, 128), bf16),
            pltpu.VMEM((2, 2, 256, 128), bf16),
            pltpu.VMEM((elems, 2, 2 * width, 128), f32),
            pltpu.VMEM((2, 2, elems, 2 * width, 128), f32),
            pltpu.VMEM((2, elems, 2 * width, 128), f32),
            pltpu.VMEM((2, elems, 2 * width, 128), f32),
            pltpu.VMEM((2, elems, 2 * width, 128), f32),
            pltpu.VMEM((2, 2, REST // 2 * width, 128), f32),
            pltpu.VMEM(table.shape, f32),
            dma((2,)), dma((2,)),
            dma((2,)), dma((2,)),
            dma((1,)), dma((1,)),
            dma((elems, 2)), dma((elems, 2)),
            dma((2,)), dma((2,)),
            dma((elems, 2)), dma((elems, 2)),
        ],
        compiler_params=pltpu.CompilerParams(
            collective_id=0, has_side_effects=True, vmem_limit_bytes=55000 * 1024
        ),
    )(hist, shapes, table)
    ordered = result.reshape(width, REST // 2, 2, RADIX).transpose(0, 2, 1, 3)
    return ordered.reshape(width, 2, REST // 2 * RADIX)


def per_device(modal_history, stress_modes):
    elems, modes = lax.axis_size("elem"), lax.axis_size("mode")
    fits = (
        elems == 8
        and modes == 4
        and modal_history.shape == (512, 128)
        and stress_modes.shape == (128, 48)
    )
    body = with_kernel if fits else plain
    return body(modal_history, stress_modes)


def solution(mesh):
    placed = (P("elem", "mode"), P("mode", "elem"))
    return jax.shard_map(
        per_device,
        mesh=mesh,
        in_specs=placed,
        out_specs=P(("elem", "mode"), None, None),
        check_vma=False,
    )
```

```python
import functools
import math

import jax
import jax.numpy as jnp
import ml_dtypes
import numpy as np
from jax import lax
from jax.experimental import pallas as pl
from jax.experimental.pallas import tpu as pltpu
from jax.sharding import PartitionSpec as P

highest = lax.Precision.HIGHEST
MESH = pl.DeviceIdType.MESH
f32, bf16 = jnp.float32, jnp.bfloat16

RADIX = 128
REST = 32


def spectra(signal):
    columns = signal.shape[0]
    radix = 64
    halved = radix // 2
    blocked = signal.reshape(columns, radix, radix)
    counter = jnp.arange(radix, dtype=jnp.int32)
    products = counter[:, None] * counter[None, :]
    small_angle = (products % radix).astype(jnp.float32) * (2.0 * math.pi / radix)
    cosine_small = jnp.cos(small_angle)
    sine_small = jnp.sin(small_angle)
    twist_angle = (products % (radix * radix)).astype(jnp.float32) * (
        2.0 * math.pi / (radix * radix)
    )
    twist_cos = jnp.cos(twist_angle)
    twist_sin = jnp.sin(twist_angle)
    first_real = jnp.einsum("cab,ak->cbk", blocked, cosine_small, precision=highest)
    first_imag = -jnp.einsum("cab,ak->cbk", blocked, sine_small, precision=highest)
    turned_real = first_real * twist_cos + first_imag * twist_sin
    turned_imag = first_imag * twist_cos - first_real * twist_sin
    cosine_half = cosine_small[:, :halved]
    sine_half = sine_small[:, :halved]
    final_real = jnp.einsum(
        "cbk,bj->cjk", turned_real, cosine_half, precision=highest
    ) + jnp.einsum("cbk,bj->cjk", turned_imag, sine_half, precision=highest)
    final_imag = jnp.einsum(
        "cbk,bj->cjk", turned_imag, cosine_half, precision=highest
    ) - jnp.einsum("cbk,bj->cjk", turned_real, sine_half, precision=highest)
    stacked = jnp.stack([final_real, final_imag], axis=1) * (1.0 / radix)
    return stacked.reshape(columns, 2, halved * radix)


def plain(modal_history, stress_modes):
    elem_count = lax.axis_size("elem")
    mode_count = lax.axis_size("mode")
    local_steps = modal_history.shape[0]
    partial_value = jnp.einsum(
        "mp,tm->pt",
        lax.all_gather(stress_modes, "elem", axis=1, tiled=True),
        modal_history,
        precision=highest,
        preferred_element_type=jnp.float32,
    )
    owned_width = partial_value.shape[0] // (elem_count * mode_count)
    reordered = partial_value.reshape(elem_count, mode_count, owned_width, local_steps)
    reordered = reordered.transpose(1, 0, 2, 3).reshape(
        mode_count * elem_count * owned_width, local_steps
    )
    summed = lax.psum_scatter(reordered, "mode", scatter_dimension=0, tiled=True)
    stress = lax.all_to_all(summed, "elem", split_axis=0, concat_axis=1, tiled=True)
    return spectra(stress)


def split_np(x):
    hi = x.astype(np.float32).astype(ml_dtypes.bfloat16)
    lo = (x - hi.astype(np.float64)).astype(np.float32).astype(ml_dtypes.bfloat16)
    return hi, lo


def tables(steps):
    two_pi = 2.0 * np.pi
    a = np.arange(RADIX)
    ang = two_pi * ((a[:, None] * a[None, :]) % RADIX) / RADIX
    parts = [np.cos(ang), -np.sin(ang)]
    k2 = np.arange(REST // 2)
    for c in range(2):
        row = np.arange(REST // 2)
        b = (2 * c + row % 2) * 8 + row // 2
        twist = two_pi * ((b[:, None] * a[None, :]) % steps) / steps
        parts += [np.cos(twist), np.sin(twist)]
        last = two_pi * ((k2[:, None] * b[None, :]) % REST) / REST
        real = np.concatenate([np.cos(last), np.sin(last)], axis=1)
        imag = np.concatenate([-np.sin(last), np.cos(last)], axis=1)
        second = np.stack([real, imag], axis=1).reshape(REST, REST) / math.sqrt(steps)
        hi, lo = (p.astype(np.float64) for p in split_np(second))
        parts.append(np.concatenate([hi, hi, lo, np.zeros_like(hi)], axis=1))
    return np.concatenate(parts, axis=0).astype(np.float32)


def split(x):
    hi = x.astype(bf16)
    lo = (x - hi.astype(f32)).astype(bf16)
    return hi, lo


def nt(a, b):
    return lax.dot_general(
        a, b, (((1,), (1,)), ((), ())), preferred_element_type=f32
    )


def nn(a, b):
    return jnp.dot(a, b, preferred_element_type=f32)


def fused(
    elems, modes, width,
    hist, shapes, table,
    out,
    hbuf, h_his, h_los, gathered, parts, other_parts, outbox, inbox,
    turned, consts,
    own_sem, fetch_sem, hs_sem, hr_sem, s1s_sem, s1r_sem, s2s_sem, s2r_sem,
    ps_sem, pr_sem, as_sem, ar_sem,
):
    chunks = 2
    e = lax.axis_index("elem")
    m = lax.axis_index("mode")
    x, core = m // 2, m % 2
    sibling = m + 1 - 2 * core
    across = (m + 2) % modes
    beside = e + 1 - 2 * (e % 2)
    halves = (x, 1 - x)
    ahead = [(e + d) % elems for d in range(elems)]
    behind = [(e + elems - d) % elems for d in range(elems)]

    fetch_shapes = pltpu.make_async_copy(
        shapes.at[x], gathered.at[e, x], fetch_sem.at[0]
    )
    fetch_table = pltpu.make_async_copy(table, consts, fetch_sem.at[1])
    own = [
        pltpu.make_async_copy(hist.at[:, c], hbuf.at[x, c], own_sem.at[c])
        for c in range(chunks)
    ]
    fetch_shapes.start()
    for copy in own:
        copy.start()
    fetch_table.start()

    barrier = pltpu.get_barrier_semaphore()
    for d in range(1, elems):
        pl.semaphore_signal(
            barrier, inc=1, device_id=(ahead[d], m), device_id_type=MESH
        )
    for peer in (across, sibling):
        pl.semaphore_signal(barrier, inc=1, device_id=(e, peer), device_id_type=MESH)
    pl.semaphore_wait(barrier, elems - 1 + 2)

    to_regroup = pltpu.make_async_remote_copy(
        shapes.at[1 - x], gathered.at[e, x], s1s_sem.at[0], s1r_sem.at[0],
        device_id=(e, across), device_id_type=MESH,
    )
    from_regroup = pltpu.make_async_remote_copy(
        shapes.at[1 - x], gathered.at[e, 1 - x], s1s_sem.at[0], s1r_sem.at[0],
        device_id=(e, across), device_id_type=MESH,
    )
    to_regroup.start()

    def shape_copy(slot, block, kind, peer):
        ref = gathered.at[block, halves[kind]]
        return pltpu.make_async_remote_copy(
            ref if kind else shapes.at[x], ref, s2s_sem.at[slot, kind], s2r_sem.at[slot, kind],
            device_id=(peer, m), device_id_type=MESH,
        )

    shape_sends = []
    order = sorted(range(1, elems), key=lambda d: -min(d, elems - d))

    def send_shapes(kind):
        for d in order:
            shape_sends.append(shape_copy(d, e, kind, ahead[d]))
            shape_sends[-1].start()

    send_shapes(0)

    to_across, from_across = [
        [
            pltpu.make_async_remote_copy(
                hist.at[:, c], hbuf.at[origin, c], hs_sem.at[c], hr_sem.at[c],
                device_id=(e, across), device_id_type=MESH,
            )
            for c in range(chunks)
        ]
        for origin in (x, 1 - x)
    ]
    for copy in to_across:
        copy.start()

    def split_history(origin, c):
        flat = hbuf.at[origin, c].reshape(256, 128)
        turned_rows = [flat[pl.ds(i, 16, stride=16), :] for i in range(16)]
        hi, lo = split(jnp.concatenate(turned_rows, axis=0))
        h_his[c, origin] = hi
        h_los[c, origin] = lo

    from_regroup.wait_recv()
    send_shapes(1)
    for c in range(chunks):
        own[c].wait()
        split_history(x, c)

    fetch_table.wait()
    w_hi, w_lo = split(
        jnp.concatenate([consts[:128, :], consts[128:256, :]], axis=1)
    )
    from_across[0].wait_recv()
    split_history(1 - x, 0)

    fetch_shapes.wait()
    for kind in range(2):
        for d in order:
            source = behind[d]
            shape_copy(d, source, kind, source).wait_recv()
    s_hi, s_lo = split(
        jnp.concatenate(
            [
                jnp.concatenate([gathered[owner, h] for h in range(2)], axis=1)
                for owner in range(elems)
            ],
            axis=0,
        )
    )
    s_both = jnp.concatenate([s_hi, s_lo], axis=0)
    rows = s_hi.shape[0]

    last_copies, part_copies = [], []
    for c in range(chunks):
        if c:
            from_across[c].wait_recv()
            split_history(1 - x, c)
        h_hi = jnp.concatenate([h_his[c, h] for h in range(2)], axis=1)
        h_lo = jnp.concatenate([h_los[c, h] for h in range(2)], axis=1)
        both = nt(s_both, h_hi)
        stress = both[:rows] + (both[rows:] + nt(s_hi, h_lo))
        for owner in range(elems):
            for k in range(2):
                for h in range(2):
                    start = (owner * 2 + k) * width
                    parts[c, k, owner, h * width : (h + 1) * width, :] = stress[
                        start : start + width, h * 128 : (h + 1) * 128
                    ]
        copy = pltpu.make_async_remote_copy(
            parts.at[c, 1 - core], other_parts.at[c], ps_sem.at[c], pr_sem.at[c],
            device_id=(e, sibling), device_id_type=MESH,
        )
        copy.start()
        part_copies.append(copy)
    for c in range(chunks):
        part_copies[c].wait_recv()
        whole = parts[c, core] + other_parts[c]
        outbox[c] = whole
        for d in order:
            peer, source = ahead[d], behind[d]
            copy = pltpu.make_async_remote_copy(
                outbox.at[c, peer], inbox.at[c, e], as_sem.at[d, c], ar_sem.at[d, c],
                device_id=(peer, m), device_id_type=MESH,
            )
            landed = pltpu.make_async_remote_copy(
                outbox.at[c, peer], inbox.at[c, source], as_sem.at[d, c],
                ar_sem.at[d, c], device_id=(peer, m), device_id_type=MESH,
            )
            copy.start()
            last_copies.append((c, copy, landed))
        inbox[c, e] = outbox[c, e]

    half = REST // 2
    total = None
    for c in range(chunks):
        for chunk, _, landed in last_copies:
            if chunk == c:
                landed.wait_recv()
        blocks = [inbox[c, i] for i in range(elems)]
        group = lax.broadcasted_iota(jnp.int32, blocks[0].shape, 1) // 16
        for step in (4, 2, 1):
            low = (group // step) % 2 == 0
            for i in range(elems):
                if (i // step) % 2 == 0:
                    one, two = blocks[i], blocks[i + step]
                    blocks[i] = jnp.where(low, one, pltpu.roll(two, 16 * step, 1))
                    blocks[i + step] = jnp.where(
                        low, pltpu.roll(one, 128 - 16 * step, 1), two
                    )
        x_hi, x_lo = split(jnp.concatenate(blocks, axis=0))
        once = nn(x_hi, w_hi) + (nn(x_lo, w_hi) + nn(x_hi, w_lo))
        turned[c, 0] = once[:, :128]
        turned[c, 1] = once[:, 128:]
        base = 256 + c * (REST + REST)
        cos = consts[base : base + half, :]
        sin = consts[base + half : base + REST, :]
        second = consts[base + REST : base + 2 * REST, : 3 * REST].astype(bf16)
        real, imag = [], []
        for col in range(width):
            re = turned.at[c, 0][pl.ds(col, half, stride=width), :]
            im = turned.at[c, 1][pl.ds(col, half, stride=width), :]
            real.append(re * cos + im * sin)
            imag.append(im * cos - re * sin)
        z = jnp.concatenate(
            [jnp.concatenate(real, axis=1), jnp.concatenate(imag, axis=1)], axis=0
        )
        z_hi, z_lo = split(z)
        part = nn(second, jnp.concatenate([z_hi, z_lo, z_hi], axis=0))
        if c == 0:
            for col in range(width):
                out[col] = part[:, col * 128 : (col + 1) * 128]
        else:
            for col in range(width):
                out[col] += part[:, col * 128 : (col + 1) * 128]

    for _, copy, _ in last_copies:
        copy.wait_send()
    for copy in [to_regroup] + shape_sends + to_across + part_copies:
        copy.wait_send()


def with_kernel(modal_history, stress_modes):
    elems, modes = lax.axis_size("elem"), lax.axis_size("mode")
    steps = modal_history.shape[0] * elems
    width = stress_modes.shape[1] // modes
    table = jnp.asarray(tables(steps))
    hist = modal_history.reshape(16, 2, 16, 128)
    shapes = stress_modes.T.reshape(2, 2 * width, 128)
    hbm = pl.BlockSpec(memory_space=pl.ANY)
    dma = pltpu.SemaphoreType.DMA
    result = pl.pallas_call(
        functools.partial(fused, elems, modes, width),
        out_shape=jax.ShapeDtypeStruct((width, REST, RADIX), f32),
        in_specs=[hbm] * 3,
        out_specs=pl.BlockSpec(memory_space=pltpu.VMEM),
        scratch_shapes=[
            pltpu.VMEM((2, 2, 16, 16, 128), f32),
            pltpu.VMEM((2, 2, 256, 128), bf16),
            pltpu.VMEM((2, 2, 256, 128), bf16),
            pltpu.VMEM((elems, 2, 2 * width, 128), f32),
            pltpu.VMEM((2, 2, elems, 2 * width, 128), f32),
            pltpu.VMEM((2, elems, 2 * width, 128), f32),
            pltpu.VMEM((2, elems, 2 * width, 128), f32),
            pltpu.VMEM((2, elems, 2 * width, 128), f32),
            pltpu.VMEM((2, 2, REST // 2 * width, 128), f32),
            pltpu.VMEM(table.shape, f32),
            dma((2,)), dma((2,)),
            dma((2,)), dma((2,)),
            dma((1,)), dma((1,)),
            dma((elems, 2)), dma((elems, 2)),
            dma((2,)), dma((2,)),
            dma((elems, 2)), dma((elems, 2)),
        ],
        compiler_params=pltpu.CompilerParams(
            collective_id=0, has_side_effects=True, vmem_limit_bytes=32 * 1024 * 1024
        ),
    )(*[pltpu.with_memory_space_constraint(a, pltpu.HBM) for a in (hist, shapes, table)])
    ordered = result.reshape(width, REST // 2, 2, RADIX).transpose(0, 2, 1, 3)
    return ordered.reshape(width, 2, REST // 2 * RADIX)


def per_device(modal_history, stress_modes):
    elems, modes = lax.axis_size("elem"), lax.axis_size("mode")
    fits = (
        elems == 8
        and modes == 4
        and modal_history.shape == (512, 128)
        and stress_modes.shape == (128, 48)
    )
    body = with_kernel if fits else plain
    return body(modal_history, stress_modes)


def solution(mesh):
    placed = (P("elem", "mode"), P("mode", "elem"))
    return jax.shard_map(
        per_device,
        mesh=mesh,
        in_specs=placed,
        out_specs=P(("elem", "mode"), None, None),
        check_vma=False,
    )
```

```python
import functools
import math

import jax
import jax.numpy as jnp
import ml_dtypes
import numpy as np
from jax import lax
from jax.experimental import pallas as pl
from jax.experimental.pallas import tpu as pltpu
from jax.sharding import PartitionSpec as P

highest = lax.Precision.HIGHEST
MESH = pl.DeviceIdType.MESH
f32, bf16 = jnp.float32, jnp.bfloat16

RADIX = 128
REST = 32


def spectra(signal):
    columns = signal.shape[0]
    radix = 64
    halved = radix // 2
    blocked = signal.reshape(columns, radix, radix)
    counter = jnp.arange(radix, dtype=jnp.int32)
    products = counter[:, None] * counter[None, :]
    small_angle = (products % radix).astype(jnp.float32) * (2.0 * math.pi / radix)
    cosine_small = jnp.cos(small_angle)
    sine_small = jnp.sin(small_angle)
    twist_angle = (products % (radix * radix)).astype(jnp.float32) * (
        2.0 * math.pi / (radix * radix)
    )
    twist_cos = jnp.cos(twist_angle)
    twist_sin = jnp.sin(twist_angle)
    first_real = jnp.einsum("cab,ak->cbk", blocked, cosine_small, precision=highest)
    first_imag = -jnp.einsum("cab,ak->cbk", blocked, sine_small, precision=highest)
    turned_real = first_real * twist_cos + first_imag * twist_sin
    turned_imag = first_imag * twist_cos - first_real * twist_sin
    cosine_half = cosine_small[:, :halved]
    sine_half = sine_small[:, :halved]
    final_real = jnp.einsum(
        "cbk,bj->cjk", turned_real, cosine_half, precision=highest
    ) + jnp.einsum("cbk,bj->cjk", turned_imag, sine_half, precision=highest)
    final_imag = jnp.einsum(
        "cbk,bj->cjk", turned_imag, cosine_half, precision=highest
    ) - jnp.einsum("cbk,bj->cjk", turned_real, sine_half, precision=highest)
    stacked = jnp.stack([final_real, final_imag], axis=1) * (1.0 / radix)
    return stacked.reshape(columns, 2, halved * radix)


def plain(modal_history, stress_modes):
    elem_count = lax.axis_size("elem")
    mode_count = lax.axis_size("mode")
    local_steps = modal_history.shape[0]
    partial_value = jnp.einsum(
        "mp,tm->pt",
        lax.all_gather(stress_modes, "elem", axis=1, tiled=True),
        modal_history,
        precision=highest,
        preferred_element_type=jnp.float32,
    )
    owned_width = partial_value.shape[0] // (elem_count * mode_count)
    reordered = partial_value.reshape(elem_count, mode_count, owned_width, local_steps)
    reordered = reordered.transpose(1, 0, 2, 3).reshape(
        mode_count * elem_count * owned_width, local_steps
    )
    summed = lax.psum_scatter(reordered, "mode", scatter_dimension=0, tiled=True)
    stress = lax.all_to_all(summed, "elem", split_axis=0, concat_axis=1, tiled=True)
    return spectra(stress)


def split_np(x):
    hi = x.astype(np.float32).astype(ml_dtypes.bfloat16)
    lo = (x - hi.astype(np.float64)).astype(np.float32).astype(ml_dtypes.bfloat16)
    return hi, lo


def tables(steps):
    two_pi = 2.0 * np.pi
    a = np.arange(RADIX)
    ang = two_pi * ((a[:, None] * a[None, :]) % RADIX) / RADIX
    parts = [np.cos(ang), -np.sin(ang)]
    k2 = np.arange(REST // 2)
    for c in range(2):
        row = np.arange(REST // 2)
        b = (2 * c + row % 2) * 8 + row // 2
        twist = two_pi * ((b[:, None] * a[None, :]) % steps) / steps
        parts += [np.cos(twist), np.sin(twist)]
        last = two_pi * ((k2[:, None] * b[None, :]) % REST) / REST
        real = np.concatenate([np.cos(last), np.sin(last)], axis=1)
        imag = np.concatenate([-np.sin(last), np.cos(last)], axis=1)
        second = np.stack([real, imag], axis=1).reshape(REST, REST) / math.sqrt(steps)
        hi, lo = (p.astype(np.float64) for p in split_np(second))
        parts.append(np.concatenate([hi, hi, lo, np.zeros_like(hi)], axis=1))
    return np.concatenate(parts, axis=0).astype(np.float32)


def split(x):
    hi = x.astype(bf16)
    lo = (x - hi.astype(f32)).astype(bf16)
    return hi, lo


def nn(a, b):
    return jnp.dot(a, b, preferred_element_type=f32)


def fused(
    elems, modes, width,
    hist, shapes, table,
    out,
    hbuf, h_his, h_los, gathered, parts, other_parts, outbox, inbox,
    turned, consts,
    own_sem, fetch_sem, hs_sem, hr_sem, s2s_sem, s2r_sem,
    ps_sem, pr_sem, as_sem, ar_sem,
):
    chunks = 2
    e = lax.axis_index("elem")
    m = lax.axis_index("mode")
    x, core = m // 2, m % 2
    sibling = m + 1 - 2 * core
    across = (m + 2) % modes
    beside = e + 1 - 2 * (e % 2)
    halves = (x, 1 - x)
    ahead = [(e + d) % elems for d in range(elems)]
    behind = [(e + elems - d) % elems for d in range(elems)]

    fetch_shapes = pltpu.make_async_copy(
        shapes.at[x], gathered.at[e, x], fetch_sem.at[0]
    )
    fetch_table = pltpu.make_async_copy(table, consts, fetch_sem.at[1])
    own = [
        pltpu.make_async_copy(hist.at[:, c], hbuf.at[x, c], own_sem.at[c])
        for c in range(chunks)
    ]
    fetch_shapes.start()
    for copy in own:
        copy.start()
    fetch_table.start()

    order = sorted(range(1, elems), key=lambda d: -min(d, elems - d))
    barrier = pltpu.get_barrier_semaphore()
    greeted = [(ahead[d], peer) for d in order for peer in (across, m)]
    greeted += [(e, across), (e, sibling)]
    for device in greeted:
        pl.semaphore_signal(barrier, inc=1, device_id=device, device_id_type=MESH)
    pl.semaphore_wait(barrier, len(greeted))

    to_across, from_across = [
        [
            pltpu.make_async_remote_copy(
                hist.at[:, c], hbuf.at[origin, c], hs_sem.at[c], hr_sem.at[c],
                device_id=(e, across), device_id_type=MESH,
            )
            for c in range(chunks)
        ]
        for origin in (x, 1 - x)
    ]
    to_across[0].start()

    shape_sends, shape_lands = [], []
    for d in order + [0]:
        for kind, side in ((0, m), (1, across)):
            if d == 0 and kind == 0:
                continue
            source = behind[d]
            send = pltpu.make_async_remote_copy(
                shapes.at[halves[kind]], gathered.at[e, x],
                s2s_sem.at[d, kind], s2r_sem.at[d, kind],
                device_id=(ahead[d], side), device_id_type=MESH,
            )
            land = pltpu.make_async_remote_copy(
                shapes.at[halves[kind]], gathered.at[source, halves[kind]],
                s2s_sem.at[d, kind], s2r_sem.at[d, kind],
                device_id=(source, side), device_id_type=MESH,
            )
            send.start()
            shape_sends.append(send)
            shape_lands.append(land)

    to_across[1].start()

    def split_history(origin, c):
        flat = hbuf.at[origin, c].reshape(256, 128)
        turned_rows = [flat[pl.ds(i, 16, stride=16), :] for i in range(16)]
        hi, lo = split(jnp.concatenate(turned_rows, axis=0).T)
        h_his[c, origin] = hi
        h_los[c, origin] = lo

    for c in range(chunks):
        own[c].wait()
        split_history(x, c)

    fetch_table.wait()
    w_hi, w_lo = split(
        jnp.concatenate([consts[:128, :], consts[128:256, :]], axis=1)
    )
    from_across[0].wait_recv()
    split_history(1 - x, 0)

    fetch_shapes.wait()
    for land in shape_lands:
        land.wait_recv()
    s_hi, s_lo = split(
        jnp.concatenate(
            [
                jnp.concatenate([gathered[owner, h] for h in range(2)], axis=1)
                for owner in range(elems)
            ],
            axis=0,
        )
    )
    s_both = jnp.concatenate([s_hi, s_lo], axis=0)
    rows = s_hi.shape[0]

    last_copies, part_copies = [], []
    for c in range(chunks):
        if c:
            from_across[c].wait_recv()
            split_history(1 - x, c)
        h_hi = jnp.concatenate([h_his[c, h] for h in range(2)], axis=0)
        h_lo = jnp.concatenate([h_los[c, h] for h in range(2)], axis=0)
        both = nn(s_both, h_hi)
        stress = both[:rows] + (both[rows:] + nn(s_hi, h_lo))
        for owner in range(elems):
            for k in range(2):
                for h in range(2):
                    start = (owner * 2 + k) * width
                    parts[c, k, owner, h * width : (h + 1) * width, :] = stress[
                        start : start + width, h * 128 : (h + 1) * 128
                    ]
        copy = pltpu.make_async_remote_copy(
            parts.at[c, 1 - core], other_parts.at[c], ps_sem.at[c], pr_sem.at[c],
            device_id=(e, sibling), device_id_type=MESH,
        )
        copy.start()
        part_copies.append(copy)
    for c in range(chunks):
        part_copies[c].wait_recv()
        whole = parts[c, core] + other_parts[c]
        outbox[c] = whole
        for d in order:
            peer, source = ahead[d], behind[d]
            copy = pltpu.make_async_remote_copy(
                outbox.at[c, peer], inbox.at[c, e], as_sem.at[d, c], ar_sem.at[d, c],
                device_id=(peer, m), device_id_type=MESH,
            )
            landed = pltpu.make_async_remote_copy(
                outbox.at[c, peer], inbox.at[c, source], as_sem.at[d, c],
                ar_sem.at[d, c], device_id=(peer, m), device_id_type=MESH,
            )
            copy.start()
            last_copies.append((c, copy, landed))
        inbox[c, e] = outbox[c, e]

    half = REST // 2
    total = None
    for c in range(chunks):
        for chunk, _, landed in last_copies:
            if chunk == c:
                landed.wait_recv()
        blocks = [inbox[c, i] for i in range(elems)]
        group = lax.broadcasted_iota(jnp.int32, blocks[0].shape, 1) // 16
        for step in (4, 2, 1):
            low = (group // step) % 2 == 0
            for i in range(elems):
                if (i // step) % 2 == 0:
                    one, two = blocks[i], blocks[i + step]
                    blocks[i] = jnp.where(low, one, pltpu.roll(two, 16 * step, 1))
                    blocks[i + step] = jnp.where(
                        low, pltpu.roll(one, 128 - 16 * step, 1), two
                    )
        x_hi, x_lo = split(jnp.concatenate(blocks, axis=0))
        once = nn(x_hi, w_hi) + (nn(x_lo, w_hi) + nn(x_hi, w_lo))
        turned[c, 0] = once[:, :128]
        turned[c, 1] = once[:, 128:]
        base = 256 + c * (REST + REST)
        cos = consts[base : base + half, :]
        sin = consts[base + half : base + REST, :]
        second = consts[base + REST : base + 2 * REST, : 3 * REST].astype(bf16)
        real, imag = [], []
        for col in range(width):
            re = turned.at[c, 0][pl.ds(col, half, stride=width), :]
            im = turned.at[c, 1][pl.ds(col, half, stride=width), :]
            real.append(re * cos + im * sin)
            imag.append(im * cos - re * sin)
        z = jnp.concatenate(
            [jnp.concatenate(real, axis=1), jnp.concatenate(imag, axis=1)], axis=0
        )
        z_hi, z_lo = split(z)
        part = nn(second, jnp.concatenate([z_hi, z_lo, z_hi], axis=0))
        if c == 0:
            for col in range(width):
                out[col] = part[:, col * 128 : (col + 1) * 128]
        else:
            for col in range(width):
                out[col] += part[:, col * 128 : (col + 1) * 128]

    for _, copy, _ in last_copies:
        copy.wait_send()
    for copy in shape_sends + to_across + part_copies:
        copy.wait_send()


def with_kernel(modal_history, stress_modes):
    elems, modes = lax.axis_size("elem"), lax.axis_size("mode")
    steps = modal_history.shape[0] * elems
    width = stress_modes.shape[1] // modes
    table = jnp.asarray(tables(steps))
    hist = modal_history.reshape(16, 2, 16, 128)
    shapes = stress_modes.T.reshape(2, 2 * width, 128)
    hbm = pl.BlockSpec(memory_space=pl.ANY)
    dma = pltpu.SemaphoreType.DMA
    result = pl.pallas_call(
        functools.partial(fused, elems, modes, width),
        out_shape=jax.ShapeDtypeStruct((width, REST, RADIX), f32),
        in_specs=[hbm] * 3,
        out_specs=pl.BlockSpec(memory_space=pltpu.VMEM),
        scratch_shapes=[
            pltpu.VMEM((2, 2, 16, 16, 128), f32),
            pltpu.VMEM((2, 2, 128, 256), bf16),
            pltpu.VMEM((2, 2, 128, 256), bf16),
            pltpu.VMEM((elems, 2, 2 * width, 128), f32),
            pltpu.VMEM((2, 2, elems, 2 * width, 128), f32),
            pltpu.VMEM((2, elems, 2 * width, 128), f32),
            pltpu.VMEM((2, elems, 2 * width, 128), f32),
            pltpu.VMEM((2, elems, 2 * width, 128), f32),
            pltpu.VMEM((2, 2, REST // 2 * width, 128), f32),
            pltpu.VMEM(table.shape, f32),
            dma((2,)), dma((2,)),
            dma((2,)), dma((2,)),
            dma((elems, 2)), dma((elems, 2)),
            dma((2,)), dma((2,)),
            dma((elems, 2)), dma((elems, 2)),
        ],
        compiler_params=pltpu.CompilerParams(
            collective_id=0, has_side_effects=True, vmem_limit_bytes=32 * 1024 * 1024
        ),
    )(*[pltpu.with_memory_space_constraint(a, pltpu.HBM) for a in (hist, shapes, table)])
    ordered = result.reshape(width, REST // 2, 2, RADIX).transpose(0, 2, 1, 3)
    return ordered.reshape(width, 2, REST // 2 * RADIX)


def per_device(modal_history, stress_modes):
    elems, modes = lax.axis_size("elem"), lax.axis_size("mode")
    fits = (
        elems == 8
        and modes == 4
        and modal_history.shape == (512, 128)
        and stress_modes.shape == (128, 48)
    )
    body = with_kernel if fits else plain
    return body(modal_history, stress_modes)


def solution(mesh):
    placed = (P("elem", "mode"), P("mode", "elem"))
    return jax.shard_map(
        per_device,
        mesh=mesh,
        in_specs=placed,
        out_specs=P(("elem", "mode"), None, None),
        check_vma=False,
    )
```

```python
import functools
import math

import jax
import jax.numpy as jnp
import ml_dtypes
import numpy as np
from jax import lax
from jax.experimental import pallas as pl
from jax.experimental.pallas import tpu as pltpu
from jax.sharding import PartitionSpec as P

highest = lax.Precision.HIGHEST
MESH = pl.DeviceIdType.MESH
f32, bf16 = jnp.float32, jnp.bfloat16

RADIX = 128
REST = 32


def spectra(signal):
    columns = signal.shape[0]
    radix = 64
    halved = radix // 2
    blocked = signal.reshape(columns, radix, radix)
    counter = jnp.arange(radix, dtype=jnp.int32)
    products = counter[:, None] * counter[None, :]
    small_angle = (products % radix).astype(jnp.float32) * (2.0 * math.pi / radix)
    cosine_small = jnp.cos(small_angle)
    sine_small = jnp.sin(small_angle)
    twist_angle = (products % (radix * radix)).astype(jnp.float32) * (
        2.0 * math.pi / (radix * radix)
    )
    twist_cos = jnp.cos(twist_angle)
    twist_sin = jnp.sin(twist_angle)
    first_real = jnp.einsum("cab,ak->cbk", blocked, cosine_small, precision=highest)
    first_imag = -jnp.einsum("cab,ak->cbk", blocked, sine_small, precision=highest)
    turned_real = first_real * twist_cos + first_imag * twist_sin
    turned_imag = first_imag * twist_cos - first_real * twist_sin
    cosine_half = cosine_small[:, :halved]
    sine_half = sine_small[:, :halved]
    final_real = jnp.einsum(
        "cbk,bj->cjk", turned_real, cosine_half, precision=highest
    ) + jnp.einsum("cbk,bj->cjk", turned_imag, sine_half, precision=highest)
    final_imag = jnp.einsum(
        "cbk,bj->cjk", turned_imag, cosine_half, precision=highest
    ) - jnp.einsum("cbk,bj->cjk", turned_real, sine_half, precision=highest)
    stacked = jnp.stack([final_real, final_imag], axis=1) * (1.0 / radix)
    return stacked.reshape(columns, 2, halved * radix)


def plain(modal_history, stress_modes):
    elem_count = lax.axis_size("elem")
    mode_count = lax.axis_size("mode")
    local_steps = modal_history.shape[0]
    partial_value = jnp.einsum(
        "mp,tm->pt",
        lax.all_gather(stress_modes, "elem", axis=1, tiled=True),
        modal_history,
        precision=highest,
        preferred_element_type=jnp.float32,
    )
    owned_width = partial_value.shape[0] // (elem_count * mode_count)
    reordered = partial_value.reshape(elem_count, mode_count, owned_width, local_steps)
    reordered = reordered.transpose(1, 0, 2, 3).reshape(
        mode_count * elem_count * owned_width, local_steps
    )
    summed = lax.psum_scatter(reordered, "mode", scatter_dimension=0, tiled=True)
    stress = lax.all_to_all(summed, "elem", split_axis=0, concat_axis=1, tiled=True)
    return spectra(stress)


def split_np(x):
    hi = x.astype(np.float32).astype(ml_dtypes.bfloat16)
    lo = (x - hi.astype(np.float64)).astype(np.float32).astype(ml_dtypes.bfloat16)
    return hi, lo


def tables(steps):
    two_pi = 2.0 * np.pi
    a = np.arange(RADIX)
    ang = two_pi * ((a[:, None] * a[None, :]) % RADIX) / RADIX
    parts = [np.cos(ang), -np.sin(ang)]
    k2 = np.arange(REST // 2)
    for c in range(2):
        row = np.arange(REST // 2)
        b = (2 * c + row % 2) * 8 + row // 2
        twist = two_pi * ((b[:, None] * a[None, :]) % steps) / steps
        parts += [np.cos(twist), np.sin(twist)]
        last = two_pi * ((k2[:, None] * b[None, :]) % REST) / REST
        real = np.concatenate([np.cos(last), np.sin(last)], axis=1)
        imag = np.concatenate([-np.sin(last), np.cos(last)], axis=1)
        second = np.stack([real, imag], axis=1).reshape(REST, REST) / math.sqrt(steps)
        hi, lo = (p.astype(np.float64) for p in split_np(second))
        parts.append(np.concatenate([hi, hi, lo, np.zeros_like(hi)], axis=1))
    return np.concatenate(parts, axis=0).astype(np.float32)


def split(x):
    hi = x.astype(bf16)
    lo = (x - hi.astype(f32)).astype(bf16)
    return hi, lo


def nn(a, b):
    return jnp.dot(a, b, preferred_element_type=f32)


def fused(
    elems, modes, width,
    hist, shapes, table,
    out,
    hbuf, h_his, h_los, mine, gathered, parts, other_parts, outbox, inbox,
    turned, consts,
    own_sem, fetch_sem, hs_sem, hr_sem, s1s_sem, s1r_sem, s2s_sem, s2r_sem,
    ps_sem, pr_sem, as_sem, ar_sem,
):
    chunks = 2
    e = lax.axis_index("elem")
    m = lax.axis_index("mode")
    x, core = m // 2, m % 2
    sibling = m + 1 - 2 * core
    across = (m + 2) % modes
    beside = e + 1 - 2 * (e % 2)
    halves = (x, 1 - x)
    ahead = [(e + d) % elems for d in range(elems)]
    behind = [(e + elems - d) % elems for d in range(elems)]

    fetch_shapes = pltpu.make_async_copy(
        shapes, mine, fetch_sem.at[0]
    )
    fetch_table = pltpu.make_async_copy(table, consts, fetch_sem.at[1])
    own = [
        pltpu.make_async_copy(hist.at[:, c], hbuf.at[x, c], own_sem.at[c])
        for c in range(chunks)
    ]
    fetch_shapes.start()
    for copy in own:
        copy.start()
    fetch_table.start()

    barrier = pltpu.get_barrier_semaphore()
    for d in range(1, elems):
        pl.semaphore_signal(
            barrier, inc=1, device_id=(ahead[d], m), device_id_type=MESH
        )
    for peer in (across, sibling):
        pl.semaphore_signal(barrier, inc=1, device_id=(e, peer), device_id_type=MESH)
    pl.semaphore_wait(barrier, elems - 1 + 2)

    to_regroup = pltpu.make_async_remote_copy(
        mine.at[1 - x], gathered.at[e, x], s1s_sem.at[0], s1r_sem.at[0],
        device_id=(e, across), device_id_type=MESH,
    )
    from_regroup = pltpu.make_async_remote_copy(
        mine.at[1 - x], gathered.at[e, 1 - x], s1s_sem.at[0], s1r_sem.at[0],
        device_id=(e, across), device_id_type=MESH,
    )
    fetch_shapes.wait()
    to_regroup.start()

    to_across, from_across = [
        [
            pltpu.make_async_remote_copy(
                hbuf.at[x, c], hbuf.at[origin, c], hs_sem.at[c], hr_sem.at[c],
                device_id=(e, across), device_id_type=MESH,
            )
            for c in range(chunks)
        ]
        for origin in (x, 1 - x)
    ]
    for c in range(chunks):
        own[c].wait()
        to_across[c].start()

    def shape_copy(slot, block, kind, peer):
        ref = gathered.at[block, halves[kind]]
        return pltpu.make_async_remote_copy(
            ref if kind else mine.at[x], ref, s2s_sem.at[slot, kind], s2r_sem.at[slot, kind],
            device_id=(peer, m), device_id_type=MESH,
        )

    shape_sends = []
    order = sorted(range(1, elems), key=lambda d: -min(d, elems - d))

    def send_shapes(kind):
        for d in order:
            shape_sends.append(shape_copy(d, e, kind, ahead[d]))
            shape_sends[-1].start()

    send_shapes(0)
    gathered[e, x] = mine[x]

    def split_history(origin, c):
        flat = hbuf.at[origin, c].reshape(256, 128)
        turned_rows = [flat[pl.ds(i, 16, stride=16), :] for i in range(16)]
        hi, lo = split(jnp.concatenate(turned_rows, axis=0).T)
        h_his[c, origin] = hi
        h_los[c, origin] = lo

    from_regroup.wait_recv()
    send_shapes(1)
    for c in range(chunks):
        split_history(x, c)

    fetch_table.wait()
    w_hi, w_lo = split(
        jnp.concatenate([consts[:128, :], consts[128:256, :]], axis=1)
    )
    from_across[0].wait_recv()
    split_history(1 - x, 0)

    for kind in range(2):
        for d in order:
            source = behind[d]
            shape_copy(d, source, kind, source).wait_recv()
    s_hi, s_lo = split(
        jnp.concatenate(
            [
                jnp.concatenate([gathered[owner, h] for h in range(2)], axis=1)
                for owner in range(elems)
            ],
            axis=0,
        )
    )
    s_both = jnp.concatenate([s_hi, s_lo], axis=0)
    rows = s_hi.shape[0]

    last_copies, part_copies = [], []
    for c in range(chunks):
        if c:
            from_across[c].wait_recv()
            split_history(1 - x, c)
        h_hi = jnp.concatenate([h_his[c, h] for h in range(2)], axis=0)
        h_lo = jnp.concatenate([h_los[c, h] for h in range(2)], axis=0)
        both = nn(s_both, h_hi)
        stress = both[:rows] + (both[rows:] + nn(s_hi, h_lo))
        for owner in range(elems):
            for k in range(2):
                for h in range(2):
                    start = (owner * 2 + k) * width
                    parts[c, k, owner, h * width : (h + 1) * width, :] = stress[
                        start : start + width, h * 128 : (h + 1) * 128
                    ]
        copy = pltpu.make_async_remote_copy(
            parts.at[c, 1 - core], other_parts.at[c], ps_sem.at[c], pr_sem.at[c],
            device_id=(e, sibling), device_id_type=MESH,
        )
        copy.start()
        part_copies.append(copy)
    for c in range(chunks):
        part_copies[c].wait_recv()
        whole = parts[c, core] + other_parts[c]
        outbox[c] = whole
        for d in order:
            peer, source = ahead[d], behind[d]
            copy = pltpu.make_async_remote_copy(
                outbox.at[c, peer], inbox.at[c, e], as_sem.at[d, c], ar_sem.at[d, c],
                device_id=(peer, m), device_id_type=MESH,
            )
            landed = pltpu.make_async_remote_copy(
                outbox.at[c, peer], inbox.at[c, source], as_sem.at[d, c],
                ar_sem.at[d, c], device_id=(peer, m), device_id_type=MESH,
            )
            copy.start()
            last_copies.append((c, copy, landed))
        inbox[c, e] = outbox[c, e]

    half = REST // 2
    total = None
    for c in range(chunks):
        for chunk, _, landed in last_copies:
            if chunk == c:
                landed.wait_recv()
        blocks = [inbox[c, i] for i in range(elems)]
        group = lax.broadcasted_iota(jnp.int32, blocks[0].shape, 1) // 16
        for step in (4, 2, 1):
            low = (group // step) % 2 == 0
            for i in range(elems):
                if (i // step) % 2 == 0:
                    one, two = blocks[i], blocks[i + step]
                    blocks[i] = jnp.where(low, one, pltpu.roll(two, 16 * step, 1))
                    blocks[i + step] = jnp.where(
                        low, pltpu.roll(one, 128 - 16 * step, 1), two
                    )
        x_hi, x_lo = split(jnp.concatenate(blocks, axis=0))
        once = nn(x_hi, w_hi) + (nn(x_lo, w_hi) + nn(x_hi, w_lo))
        turned[c, 0] = once[:, :128]
        turned[c, 1] = once[:, 128:]
        base = 256 + c * (REST + REST)
        cos = consts[base : base + half, :]
        sin = consts[base + half : base + REST, :]
        second = consts[base + REST : base + 2 * REST, : 3 * REST].astype(bf16)
        real, imag = [], []
        for col in range(width):
            re = turned.at[c, 0][pl.ds(col, half, stride=width), :]
            im = turned.at[c, 1][pl.ds(col, half, stride=width), :]
            real.append(re * cos + im * sin)
            imag.append(im * cos - re * sin)
        z = jnp.concatenate(
            [jnp.concatenate(real, axis=1), jnp.concatenate(imag, axis=1)], axis=0
        )
        z_hi, z_lo = split(z)
        part = nn(second, jnp.concatenate([z_hi, z_lo, z_hi], axis=0))
        if c == 0:
            for col in range(width):
                out[col] = part[:, col * 128 : (col + 1) * 128]
        else:
            for col in range(width):
                out[col] += part[:, col * 128 : (col + 1) * 128]

    for _, copy, _ in last_copies:
        copy.wait_send()
    for copy in [to_regroup] + shape_sends + to_across + part_copies:
        copy.wait_send()


def with_kernel(modal_history, stress_modes):
    elems, modes = lax.axis_size("elem"), lax.axis_size("mode")
    steps = modal_history.shape[0] * elems
    width = stress_modes.shape[1] // modes
    table = jnp.asarray(tables(steps))
    hist = modal_history.reshape(16, 2, 16, 128)
    shapes = stress_modes.T.reshape(2, 2 * width, 128)
    hbm = pl.BlockSpec(memory_space=pl.ANY)
    dma = pltpu.SemaphoreType.DMA
    result = pl.pallas_call(
        functools.partial(fused, elems, modes, width),
        out_shape=jax.ShapeDtypeStruct((width, REST, RADIX), f32),
        in_specs=[hbm] * 3,
        out_specs=pl.BlockSpec(memory_space=pltpu.VMEM),
        scratch_shapes=[
            pltpu.VMEM((2, 2, 16, 16, 128), f32),
            pltpu.VMEM((2, 2, 128, 256), bf16),
            pltpu.VMEM((2, 2, 128, 256), bf16),
            pltpu.VMEM((2, 2 * width, 128), f32),
            pltpu.VMEM((elems, 2, 2 * width, 128), f32),
            pltpu.VMEM((2, 2, elems, 2 * width, 128), f32),
            pltpu.VMEM((2, elems, 2 * width, 128), f32),
            pltpu.VMEM((2, elems, 2 * width, 128), f32),
            pltpu.VMEM((2, elems, 2 * width, 128), f32),
            pltpu.VMEM((2, 2, REST // 2 * width, 128), f32),
            pltpu.VMEM(table.shape, f32),
            dma((2,)), dma((2,)),
            dma((2,)), dma((2,)),
            dma((1,)), dma((1,)),
            dma((elems, 2)), dma((elems, 2)),
            dma((2,)), dma((2,)),
            dma((elems, 2)), dma((elems, 2)),
        ],
        compiler_params=pltpu.CompilerParams(
            collective_id=0, has_side_effects=True, vmem_limit_bytes=32 * 1024 * 1024
        ),
    )(*[pltpu.with_memory_space_constraint(a, pltpu.HBM) for a in (hist, shapes, table)])
    ordered = result.reshape(width, REST // 2, 2, RADIX).transpose(0, 2, 1, 3)
    return ordered.reshape(width, 2, REST // 2 * RADIX)


def per_device(modal_history, stress_modes):
    elems, modes = lax.axis_size("elem"), lax.axis_size("mode")
    fits = (
        elems == 8
        and modes == 4
        and modal_history.shape == (512, 128)
        and stress_modes.shape == (128, 48)
    )
    body = with_kernel if fits else plain
    return body(modal_history, stress_modes)


def solution(mesh):
    placed = (P("elem", "mode"), P("mode", "elem"))
    return jax.shard_map(
        per_device,
        mesh=mesh,
        in_specs=placed,
        out_specs=P(("elem", "mode"), None, None),
        check_vma=False,
    )
```

```python
import functools
import math

import jax
import jax.numpy as jnp
import ml_dtypes
import numpy as np
from jax import lax
from jax.experimental import pallas as pl
from jax.experimental.pallas import tpu as pltpu
from jax.sharding import PartitionSpec as P

highest = lax.Precision.HIGHEST
MESH = pl.DeviceIdType.MESH
f32, bf16 = jnp.float32, jnp.bfloat16

RADIX = 128
REST = 32


def spectra(signal):
    columns = signal.shape[0]
    radix = 64
    halved = radix // 2
    blocked = signal.reshape(columns, radix, radix)
    counter = jnp.arange(radix, dtype=jnp.int32)
    products = counter[:, None] * counter[None, :]
    small_angle = (products % radix).astype(jnp.float32) * (2.0 * math.pi / radix)
    cosine_small = jnp.cos(small_angle)
    sine_small = jnp.sin(small_angle)
    twist_angle = (products % (radix * radix)).astype(jnp.float32) * (
        2.0 * math.pi / (radix * radix)
    )
    twist_cos = jnp.cos(twist_angle)
    twist_sin = jnp.sin(twist_angle)
    first_real = jnp.einsum("cab,ak->cbk", blocked, cosine_small, precision=highest)
    first_imag = -jnp.einsum("cab,ak->cbk", blocked, sine_small, precision=highest)
    turned_real = first_real * twist_cos + first_imag * twist_sin
    turned_imag = first_imag * twist_cos - first_real * twist_sin
    cosine_half = cosine_small[:, :halved]
    sine_half = sine_small[:, :halved]
    final_real = jnp.einsum(
        "cbk,bj->cjk", turned_real, cosine_half, precision=highest
    ) + jnp.einsum("cbk,bj->cjk", turned_imag, sine_half, precision=highest)
    final_imag = jnp.einsum(
        "cbk,bj->cjk", turned_imag, cosine_half, precision=highest
    ) - jnp.einsum("cbk,bj->cjk", turned_real, sine_half, precision=highest)
    stacked = jnp.stack([final_real, final_imag], axis=1) * (1.0 / radix)
    return stacked.reshape(columns, 2, halved * radix)


def plain(modal_history, stress_modes):
    elem_count = lax.axis_size("elem")
    mode_count = lax.axis_size("mode")
    local_steps = modal_history.shape[0]
    partial_value = jnp.einsum(
        "mp,tm->pt",
        lax.all_gather(stress_modes, "elem", axis=1, tiled=True),
        modal_history,
        precision=highest,
        preferred_element_type=jnp.float32,
    )
    owned_width = partial_value.shape[0] // (elem_count * mode_count)
    reordered = partial_value.reshape(elem_count, mode_count, owned_width, local_steps)
    reordered = reordered.transpose(1, 0, 2, 3).reshape(
        mode_count * elem_count * owned_width, local_steps
    )
    summed = lax.psum_scatter(reordered, "mode", scatter_dimension=0, tiled=True)
    stress = lax.all_to_all(summed, "elem", split_axis=0, concat_axis=1, tiled=True)
    return spectra(stress)


def split_np(x):
    hi = x.astype(np.float32).astype(ml_dtypes.bfloat16)
    lo = (x - hi.astype(np.float64)).astype(np.float32).astype(ml_dtypes.bfloat16)
    return hi, lo


def tables(steps):
    two_pi = 2.0 * np.pi
    a = np.arange(RADIX)
    ang = two_pi * ((a[:, None] * a[None, :]) % RADIX) / RADIX
    parts = [np.cos(ang), -np.sin(ang)]
    k2 = np.arange(REST // 2)
    for c in range(2):
        row = np.arange(REST // 2)
        b = (2 * c + row % 2) * 8 + row // 2
        twist = two_pi * ((b[:, None] * a[None, :]) % steps) / steps
        parts += [np.cos(twist), np.sin(twist)]
        last = two_pi * ((k2[:, None] * b[None, :]) % REST) / REST
        real = np.concatenate([np.cos(last), np.sin(last)], axis=1)
        imag = np.concatenate([-np.sin(last), np.cos(last)], axis=1)
        second = np.stack([real, imag], axis=1).reshape(REST, REST) / math.sqrt(steps)
        hi, lo = (p.astype(np.float64) for p in split_np(second))
        parts.append(np.concatenate([hi, hi, lo, np.zeros_like(hi)], axis=1))
    return np.concatenate(parts, axis=0).astype(np.float32)


def split(x):
    hi = x.astype(bf16)
    lo = (x - hi.astype(f32)).astype(bf16)
    return hi, lo


def nn(a, b):
    return jnp.dot(a, b, preferred_element_type=f32)


def fused(
    elems, modes, width,
    hist, shapes, table,
    out,
    hbuf, h_his, h_los, mine, gathered, parts, other_parts, outbox, inbox,
    turned, consts,
    own_sem, fetch_sem, hs_sem, hr_sem, s1s_sem, s1r_sem, s2s_sem, s2r_sem,
    ps_sem, pr_sem, as_sem, ar_sem,
):
    chunks = 2
    e = lax.axis_index("elem")
    m = lax.axis_index("mode")
    x, core = m // 2, m % 2
    sibling = m + 1 - 2 * core
    across = (m + 2) % modes
    halves = (x, 1 - x)
    flips = [1 - 2 * (e % 2), 2 - 4 * (e // 2 % 2), 4 - 8 * (e // 4)]
    partner = [
        e + sum(flips[i] for i in range(3) if d // 2**i % 2) for d in range(elems)
    ]
    order = range(elems - 1, 0, -1)

    fetch_shapes = pltpu.make_async_copy(
        shapes, mine, fetch_sem.at[0]
    )
    fetch_table = pltpu.make_async_copy(table, consts, fetch_sem.at[1])
    own = [
        pltpu.make_async_copy(hist.at[:, c], hbuf.at[x, c], own_sem.at[c])
        for c in range(chunks)
    ]
    fetch_shapes.start()
    for copy in own:
        copy.start()
    fetch_table.start()

    barrier = pltpu.get_barrier_semaphore()
    for d in order:
        pl.semaphore_signal(
            barrier, inc=1, device_id=(partner[d], m), device_id_type=MESH
        )
    for peer in (across, sibling):
        pl.semaphore_signal(barrier, inc=1, device_id=(e, peer), device_id_type=MESH)
    pl.semaphore_wait(barrier, elems - 1 + 2)

    to_regroup = pltpu.make_async_remote_copy(
        mine.at[1 - x], gathered.at[e, x], s1s_sem.at[0], s1r_sem.at[0],
        device_id=(e, across), device_id_type=MESH,
    )
    from_regroup = pltpu.make_async_remote_copy(
        mine.at[1 - x], gathered.at[e, 1 - x], s1s_sem.at[0], s1r_sem.at[0],
        device_id=(e, across), device_id_type=MESH,
    )
    fetch_shapes.wait()
    to_regroup.start()

    to_across, from_across = [
        [
            pltpu.make_async_remote_copy(
                hbuf.at[x, c], hbuf.at[origin, c], hs_sem.at[c], hr_sem.at[c],
                device_id=(e, across), device_id_type=MESH,
            )
            for c in range(chunks)
        ]
        for origin in (x, 1 - x)
    ]
    for c in range(chunks):
        own[c].wait()
        to_across[c].start()

    def shape_copy(slot, block, kind, peer):
        ref = gathered.at[block, halves[kind]]
        return pltpu.make_async_remote_copy(
            ref if kind else mine.at[x], ref, s2s_sem.at[slot, kind], s2r_sem.at[slot, kind],
            device_id=(peer, m), device_id_type=MESH,
        )

    shape_sends = []

    def send_shapes(kind):
        for d in order:
            shape_sends.append(shape_copy(d, e, kind, partner[d]))
            shape_sends[-1].start()

    send_shapes(0)
    gathered[e, x] = mine[x]

    def split_history(origin, c):
        flat = hbuf.at[origin, c].reshape(256, 128)
        turned_rows = [flat[pl.ds(i, 16, stride=16), :] for i in range(16)]
        hi, lo = split(jnp.concatenate(turned_rows, axis=0).T)
        h_his[c, origin] = hi
        h_los[c, origin] = lo

    from_regroup.wait_recv()
    send_shapes(1)
    for c in range(chunks):
        split_history(x, c)

    fetch_table.wait()
    w_hi, w_lo = split(
        jnp.concatenate([consts[:128, :], consts[128:256, :]], axis=1)
    )
    from_across[0].wait_recv()
    split_history(1 - x, 0)

    for kind in range(2):
        for d in order:
            source = partner[d]
            shape_copy(d, source, kind, source).wait_recv()
    s_hi, s_lo = split(
        jnp.concatenate(
            [
                jnp.concatenate([gathered[owner, h] for h in range(2)], axis=1)
                for owner in range(elems)
            ],
            axis=0,
        )
    )
    s_both = jnp.concatenate([s_hi, s_lo], axis=0)
    rows = s_hi.shape[0]

    last_copies, part_copies = [], []
    for c in range(chunks):
        if c:
            from_across[c].wait_recv()
            split_history(1 - x, c)
        h_hi = jnp.concatenate([h_his[c, h] for h in range(2)], axis=0)
        h_lo = jnp.concatenate([h_los[c, h] for h in range(2)], axis=0)
        both = nn(s_both, h_hi)
        stress = both[:rows] + (both[rows:] + nn(s_hi, h_lo))
        for owner in range(elems):
            for k in range(2):
                for h in range(2):
                    start = (owner * 2 + k) * width
                    parts[c, k, owner, h * width : (h + 1) * width, :] = stress[
                        start : start + width, h * 128 : (h + 1) * 128
                    ]
        copy = pltpu.make_async_remote_copy(
            parts.at[c, 1 - core], other_parts.at[c], ps_sem.at[c], pr_sem.at[c],
            device_id=(e, sibling), device_id_type=MESH,
        )
        copy.start()
        part_copies.append(copy)
    for c in range(chunks):
        part_copies[c].wait_recv()
        whole = parts[c, core] + other_parts[c]
        outbox[c] = whole
        for d in order:
            peer, source = partner[d], partner[d]
            copy = pltpu.make_async_remote_copy(
                outbox.at[c, peer], inbox.at[c, e], as_sem.at[d, c], ar_sem.at[d, c],
                device_id=(peer, m), device_id_type=MESH,
            )
            landed = pltpu.make_async_remote_copy(
                outbox.at[c, peer], inbox.at[c, source], as_sem.at[d, c],
                ar_sem.at[d, c], device_id=(peer, m), device_id_type=MESH,
            )
            copy.start()
            last_copies.append((c, copy, landed))
        inbox[c, e] = outbox[c, e]

    half = REST // 2
    total = None
    for c in range(chunks):
        for chunk, _, landed in last_copies:
            if chunk == c:
                landed.wait_recv()
        blocks = [inbox[c, i] for i in range(elems)]
        group = lax.broadcasted_iota(jnp.int32, blocks[0].shape, 1) // 16
        for step in (4, 2, 1):
            low = (group // step) % 2 == 0
            for i in range(elems):
                if (i // step) % 2 == 0:
                    one, two = blocks[i], blocks[i + step]
                    blocks[i] = jnp.where(low, one, pltpu.roll(two, 16 * step, 1))
                    blocks[i + step] = jnp.where(
                        low, pltpu.roll(one, 128 - 16 * step, 1), two
                    )
        x_hi, x_lo = split(jnp.concatenate(blocks, axis=0))
        once = nn(x_hi, w_hi) + (nn(x_lo, w_hi) + nn(x_hi, w_lo))
        turned[c, 0] = once[:, :128]
        turned[c, 1] = once[:, 128:]
        base = 256 + c * (REST + REST)
        cos = consts[base : base + half, :]
        sin = consts[base + half : base + REST, :]
        second = consts[base + REST : base + 2 * REST, : 3 * REST].astype(bf16)
        real, imag = [], []
        for col in range(width):
            re = turned.at[c, 0][pl.ds(col, half, stride=width), :]
            im = turned.at[c, 1][pl.ds(col, half, stride=width), :]
            real.append(re * cos + im * sin)
            imag.append(im * cos - re * sin)
        z = jnp.concatenate(
            [jnp.concatenate(real, axis=1), jnp.concatenate(imag, axis=1)], axis=0
        )
        z_hi, z_lo = split(z)
        part = nn(second, jnp.concatenate([z_hi, z_lo, z_hi], axis=0))
        if c == 0:
            for col in range(width):
                out[col] = part[:, col * 128 : (col + 1) * 128]
        else:
            for col in range(width):
                out[col] += part[:, col * 128 : (col + 1) * 128]

    for _, copy, _ in last_copies:
        copy.wait_send()
    for copy in [to_regroup] + shape_sends + to_across + part_copies:
        copy.wait_send()


def with_kernel(modal_history, stress_modes):
    elems, modes = lax.axis_size("elem"), lax.axis_size("mode")
    steps = modal_history.shape[0] * elems
    width = stress_modes.shape[1] // modes
    table = jnp.asarray(tables(steps))
    hist = modal_history.reshape(16, 2, 16, 128)
    shapes = stress_modes.T.reshape(2, 2 * width, 128)
    hbm = pl.BlockSpec(memory_space=pl.ANY)
    dma = pltpu.SemaphoreType.DMA
    result = pl.pallas_call(
        functools.partial(fused, elems, modes, width),
        out_shape=jax.ShapeDtypeStruct((width, REST, RADIX), f32),
        in_specs=[hbm] * 3,
        out_specs=pl.BlockSpec(memory_space=pltpu.VMEM),
        scratch_shapes=[
            pltpu.VMEM((2, 2, 16, 16, 128), f32),
            pltpu.VMEM((2, 2, 128, 256), bf16),
            pltpu.VMEM((2, 2, 128, 256), bf16),
            pltpu.VMEM((2, 2 * width, 128), f32),
            pltpu.VMEM((elems, 2, 2 * width, 128), f32),
            pltpu.VMEM((2, 2, elems, 2 * width, 128), f32),
            pltpu.VMEM((2, elems, 2 * width, 128), f32),
            pltpu.VMEM((2, elems, 2 * width, 128), f32),
            pltpu.VMEM((2, elems, 2 * width, 128), f32),
            pltpu.VMEM((2, 2, REST // 2 * width, 128), f32),
            pltpu.VMEM(table.shape, f32),
            dma((2,)), dma((2,)),
            dma((2,)), dma((2,)),
            dma((1,)), dma((1,)),
            dma((elems, 2)), dma((elems, 2)),
            dma((2,)), dma((2,)),
            dma((elems, 2)), dma((elems, 2)),
        ],
        compiler_params=pltpu.CompilerParams(
            collective_id=0, has_side_effects=True, vmem_limit_bytes=32 * 1024 * 1024
        ),
    )(*[pltpu.with_memory_space_constraint(a, pltpu.HBM) for a in (hist, shapes, table)])
    ordered = result.reshape(width, REST // 2, 2, RADIX).transpose(0, 2, 1, 3)
    return ordered.reshape(width, 2, REST // 2 * RADIX)


def per_device(modal_history, stress_modes):
    elems, modes = lax.axis_size("elem"), lax.axis_size("mode")
    fits = (
        elems == 8
        and modes == 4
        and modal_history.shape == (512, 128)
        and stress_modes.shape == (128, 48)
    )
    body = with_kernel if fits else plain
    return body(modal_history, stress_modes)


def solution(mesh):
    placed = (P("elem", "mode"), P("mode", "elem"))
    return jax.shard_map(
        per_device,
        mesh=mesh,
        in_specs=placed,
        out_specs=P(("elem", "mode"), None, None),
        check_vma=False,
    )
```
